512 devices in a mesh: row: 8 (over z_lo), col: 4 (over x), blk: 16 (over z_hi, y, core).
Axes of the slice: x: 4, y: 4, z: 16 (z_hi: 2, z_lo: 8; z = z_hi * 8 + z_lo), core: 2. Of those that a mesh axis runs over, the one named last changes fastest.
Arguments:
- theta: float32 [64, 256, 1024], P('blk', 'row', 'col'), may hold values from -6 to 6
- section: float32 [64, 256, 1024], P('blk', 'row', 'col'), may hold values from -6 to 6
- velocity: float32 [3, 32, 128, 512], P(None, None, ('row', 'blk'), 'col'), may hold values from -6 to 6
- lower_plane: int32 [64], replicated, may hold values from 0 to 30, as said below
- weight_x: float32 [64], P('blk'), may hold values from 0 to 1
- metric_x: float32 [64], P('blk'), may hold values from 0.5 to 2
- first_x: float32 [4, 4], replicated
- first_y: float32 [32, 32], replicated
- first_z: float32 [256, 256], replicated
- second_x: float32 [4, 4], replicated
- second_y: float32 [32, 32], replicated
- second_z: float32 [256, 256], replicated
Outputs:
- theta_new: float32 [64, 256, 1024], P('blk', 'row', 'col')
- section_new: float32 [64, 256, 1024], P('blk', 'row', 'col')
The draws below stay inside these ranges and needn't reach their ends.
Inputs may be any that keep to these rules, and one draw needn't show every extreme that they name: lower_plane[i] differs from i // 2 by at most one; in every aligned block of 4 fine planes the planes lower_plane[i] and lower_plane[i] + 1 lie within 5 consecutive coarse planes, and some block needs all 5.
All inputs are finite; a program needn't handle non-finite values.
Results may differ from the reference program's by a relative error of at most 0.00005.
Values sent between devices are 32-bit elements; how exact they have to be, the bound alone decides.
A program may use at most 64 MiB of HBM per device.

```python
import math
import jax
import jax.numpy as jnp
from jax import lax

BX = 4
BY = 32
BZ = 256
NX = 64
NY = 256
NZ = 1024
VX = 32
VY = 128
VZ = 512


def unit_diagonal(key, extent, spread):
    jitter = jnp.clip(jax.random.normal(key, (extent, extent), jnp.float32), -4.0, 4.0)
    return jnp.eye(extent, dtype=jnp.float32) + jitter * (spread / extent ** 0.5)


def draw_lower_plane(key, part):
    key = jax.random.fold_in(key, 11)
    key_jitter, key_block = jax.random.split(key)
    block_count = NX // BX
    positions = jnp.arange(NX, dtype=jnp.int32)
    jitter = jax.random.randint(key_jitter, (NX,), -1, 2, dtype=jnp.int32)
    planes = positions // 2 + jitter
    chosen = jax.random.randint(key_block, (), 1, block_count - 1, dtype=jnp.int32)
    first_cell = chosen * BX
    planes = jnp.where(positions == first_cell, positions // 2 - 1, planes)
    planes = jnp.where(positions == first_cell + BX - 1, positions // 2 + 1, planes)
    planes = jnp.where(positions == 0, 0, planes)
    return jnp.clip(planes, 0, NX // 2 - 2).astype(jnp.int32)


def draw_first_x(key, part):
    key = jax.random.fold_in(key, 21)
    return unit_diagonal(key, BX, 0.5)


def draw_first_y(key, part):
    key = jax.random.fold_in(key, 22)
    return unit_diagonal(key, BY, 0.5)


def draw_first_z(key, part):
    key = jax.random.fold_in(key, 23)
    return unit_diagonal(key, BZ, 0.5)


def draw_second_x(key, part):
    key = jax.random.fold_in(key, 24)
    return unit_diagonal(key, BX, 0.5)


def draw_second_y(key, part):
    key = jax.random.fold_in(key, 25)
    return unit_diagonal(key, BY, 0.5)


def draw_second_z(key, part):
    key = jax.random.fold_in(key, 26)
    return unit_diagonal(key, BZ, 0.5)


def steps_of(stream_key, shape, shards, smallest, high):
    factor_of = 1.0
    for position, parts in shards:
        steps = jax.random.uniform(jax.random.fold_in(jax.random.fold_in(stream_key, 6), position), (parts,), jnp.float32, smallest / len(shards), high / len(shards))
        factor_of = factor_of * jnp.repeat(jnp.exp(steps), shape[position] // parts).reshape((-1,) + (1,) * (len(shape) - 1 - position))
    return factor_of


def centred(own_key, shape, scale, reach, cuts=(), kind=jnp.bfloat16):
    values = jax.random.normal(own_key, shape, jnp.float32) * scale
    if len(cuts) > 0:
        values = steps_of(own_key, shape, cuts, -0.22, 0.18) * values
    return jnp.clip(values, min=-reach, max=reach).astype(kind)


def setup_inputs(seed: int = 0) -> dict:
    keys = jax.random.split(jax.random.key(seed), 13)
    theta = centred(keys[0], (NX, NY, NZ), 1.0, 6.0, ((0, 16), (1, 8), (2, 4)), jnp.float32)
    section = centred(keys[1], (NX, NY, NZ), 1.0, 6.0, ((0, 16), (1, 8), (2, 4)), jnp.float32)
    velocity = centred(keys[2], (3, VX, VY, VZ), 1.0, 6.0, ((2, 128), (3, 4)), jnp.float32)
    lower_plane = draw_lower_plane(jax.random.fold_in(keys[12], 71), 0)
    weight_x = jnp.clip(1.0 * jax.random.uniform(keys[4], (NX,), jnp.float32) ** steps_of(keys[4], (NX,), ((0, 16),), -0.2, 0.2), 0.0, 1.0)
    metric_x = jnp.clip(jnp.exp(math.log(2.0) - 1.3862944 * jax.random.uniform(keys[5], (NX,), jnp.float32) ** steps_of(keys[5], (NX,), ((0, 16),), -0.2, 0.2)), 0.5, 2.0)
    first_x = draw_first_x(jax.random.fold_in(keys[12], 71), 0)
    first_y = draw_first_y(jax.random.fold_in(keys[12], 71), 0)
    first_z = draw_first_z(jax.random.fold_in(keys[12], 71), 0)
    second_x = draw_second_x(jax.random.fold_in(keys[12], 71), 0)
    second_y = draw_second_y(jax.random.fold_in(keys[12], 71), 0)
    second_z = draw_second_z(jax.random.fold_in(keys[12], 71), 0)
    return {"theta": theta, "section": section, "velocity": velocity, "lower_plane": lower_plane, "weight_x": weight_x, "metric_x": metric_x, "first_x": first_x, "first_y": first_y, "first_z": first_z, "second_x": second_x, "second_y": second_y, "second_z": second_z}


HIGHEST_PRECISION = lax.Precision.HIGHEST
TIME_STEP = 0.2
DIFFUSIVITY = 0.2
MEAN_GRADIENT = 1.0
SECTION_DECAY = -5.0 / 9.0
SECTION_WEIGHT = 15.0 / 16.0


def shifted(values, offset, axis_index):
    return jnp.roll(values, -offset, axis_index)


def first_rhs(values, axis_index):
    return (7.0 / 9.0) * (shifted(values, 1, axis_index) - shifted(values, -1, axis_index)) + (1.0 / 36.0) * (
        shifted(values, 2, axis_index) - shifted(values, -2, axis_index))


def second_rhs(values, axis_index):
    return (12.0 / 11.0) * (shifted(values, 1, axis_index) - 2.0 * values + shifted(values, -1, axis_index)) + (
        3.0 / 44.0) * (shifted(values, 2, axis_index) - 2.0 * values + shifted(values, -2, axis_index))


def along_blocks(matrix, values, axis_index):
    extent = matrix.shape[0]
    full_shape = values.shape
    if axis_index == 0:
        blocked = values.reshape(full_shape[0] // extent, extent, full_shape[1], full_shape[2])
        result = jnp.einsum("ij,bjyz->biyz", matrix, blocked, precision=HIGHEST_PRECISION)
    elif axis_index == 1:
        blocked = values.reshape(full_shape[0], full_shape[1] // extent, extent, full_shape[2])
        result = jnp.einsum("ij,xbjz->xbiz", matrix, blocked, precision=HIGHEST_PRECISION)
    else:
        blocked = values.reshape(full_shape[0], full_shape[1], full_shape[2] // extent, extent)
        result = jnp.einsum("ij,xybj->xybi", matrix, blocked, precision=HIGHEST_PRECISION)
    return result.reshape(full_shape)


def refine_along(coarse, axis_index):
    even_cells = 0.75 * coarse + 0.25 * jnp.roll(coarse, 1, axis_index)
    odd_cells = 0.75 * coarse + 0.25 * jnp.roll(coarse, -1, axis_index)
    stacked = jnp.stack([even_cells, odd_cells], axis=axis_index + 1)
    new_shape = list(coarse.shape)
    new_shape[axis_index] = 2 * coarse.shape[axis_index]
    return stacked.reshape(new_shape)


def reference(theta, section, velocity, lower_plane, weight_x, metric_x, first_x, first_y, first_z, second_x,
              second_y, second_z):
    fraction = weight_x[None, :, None, None]
    lower_planes = jnp.take(velocity, lower_plane, axis=1)
    upper_planes = jnp.take(velocity, lower_plane + 1, axis=1)
    planes = (1.0 - fraction) * lower_planes + fraction * upper_planes
    refined = refine_along(refine_along(planes, 2), 3)
    flow_x = refined[0]
    flow_y = refined[1]
    flow_z = refined[2]
    stretch = metric_x[:, None, None]
    slope_x = stretch * along_blocks(first_x, first_rhs(theta, 0), 0)
    slope_y = along_blocks(first_y, first_rhs(theta, 1), 1)
    slope_z = along_blocks(first_z, first_rhs(theta, 2), 2)
    divergence = stretch * along_blocks(first_x, first_rhs(flow_x * theta, 0), 0) + along_blocks(
        first_y, first_rhs(flow_y * theta, 1), 1) + along_blocks(first_z, first_rhs(flow_z * theta, 2), 2)
    advect = 0.5 * (flow_x * slope_x + flow_y * slope_y + flow_z * slope_z + divergence)
    laplace = stretch * stretch * along_blocks(second_x, second_rhs(theta, 0), 0) + along_blocks(
        second_y, second_rhs(theta, 1), 1) + along_blocks(second_z, second_rhs(theta, 2), 2)
    tendency = -advect - MEAN_GRADIENT * flow_y + DIFFUSIVITY * laplace
    section_new = SECTION_DECAY * section + TIME_STEP * tendency
    theta_new = theta + SECTION_WEIGHT * section_new
    return theta_new, section_new
```

```python
import jax
import jax.numpy as jnp
from jax import lax
from jax.experimental import pallas as pl
from jax.experimental.pallas import tpu as pltpu
from jax.sharding import PartitionSpec as P

F32 = jnp.float32
BF16 = jnp.bfloat16
SLAB = 24
NN = (((1,), (0,)), ((), ()))
NT = (((1,), (1,)), ((), ()))


def split2(x):
    high = x.astype(BF16)
    return high, (x - high.astype(F32)).astype(BF16)


def split3(x):
    high = x.astype(BF16)
    rest = x - high.astype(F32)
    mid = rest.astype(BF16)
    return high, mid, (rest - mid.astype(F32)).astype(BF16)


def dot(a, b, dims=NN):
    return lax.dot_general(a, b, dims, preferred_element_type=F32)


def iota(shape, dim):
    return lax.broadcasted_iota(jnp.int32, shape, dim)


def first_weights(d):
    zero = jnp.zeros(d.shape, F32)
    return jnp.where(
        d == 1, 28.0, jnp.where(d == -1, -28.0, jnp.where(d == 2, 1.0, jnp.where(d == -2, -1.0, zero)))
    ).astype(BF16)


def second_weights(d):
    zero = jnp.zeros(d.shape, F32)
    far = jnp.abs(d)
    return jnp.where(
        far == 0, -102.0, jnp.where(far == 1, 48.0, jnp.where(far == 2, 3.0, zero))
    ).astype(BF16)


def kernel(
    lower, weight, metric, fx, sx,
    theta_in, vel_in, fy_in, sy_in, fz_in, sz_in,
    out_ref,
    theta, vel, fy, sy, fz, sz,
    xlo, xhi, wown, wlo, whi, ypack, yrecv, zpack, zrecv, vzpack, vzrecv,
    pack, buf, coef, mix, rz, m1h, m1l, m2h, m2l, my, tpad, vt, fine0, fine1, fine2, efine,
    gx, gy, gz, lap,
    in_sem, x_send, x_recv, w_send, w_recv, y_send, y_recv, z_send, z_recv, v_send, v_recv,
    a_send, a_recv, b_send, b_recv, p_send, p_recv, r_send, r_recv,
):
    row, col, blk = lax.axis_index("row"), lax.axis_index("col"), lax.axis_index("blk")
    rows, cols = lax.axis_size("row"), lax.axis_size("col")
    chip, core = blk // 2, blk % 2
    zhi, ypos = chip // 4, chip % 4

    loads = []
    for n, (src, dst) in enumerate(
        ((vel_in, vel.at[pl.ds(0, 96)]), (theta_in, theta), (fz_in, fz), (sz_in, sz), (fy_in, fy), (sy_in, sy))
    ):
        load = pltpu.make_async_copy(src, dst, in_sem.at[n])
        load.start()
        loads.append(load)

    partner = {"blk": 2 * chip + (1 - core)}
    outer = {"blk": (blk + 2 * core + 15) % 16}
    up_blk, down_blk = {"blk": (blk + 1) % 16}, {"blk": (blk + 15) % 16}
    up_row, down_row = {"row": (row + 1) % rows}, {"row": (row + rows - 1) % rows}
    up_col, down_col = {"col": (col + 1) % cols}, {"col": (col + cols - 1) % cols}
    chips, senders = [], []
    for far, dy in ((1, 0), (1, 1), (1, 2), (1, 3), (0, 1), (0, 2), (0, 3)):
        chips.append(((zhi + far) % 2) * 4 + (ypos + dy) % 4)
        senders.append(((zhi + far) % 2) * 4 + (ypos + 4 - dy) % 4)

    barrier = pltpu.get_barrier_semaphore()
    peers = [{"blk": 2 * q + core} for q in chips] + [partner, outer, up_row, down_row, up_col, down_col]
    for peer in peers:
        pl.semaphore_signal(barrier, inc=1, device_id=peer, device_id_type=pl.DeviceIdType.MESH)

    started = []

    def send(src, dst, ssem, rsem, device):
        copy = pltpu.make_async_remote_copy(
            src_ref=src, dst_ref=dst, send_sem=ssem, recv_sem=rsem,
            device_id=device, device_id_type=pl.DeviceIdType.MESH,
        )
        copy.start()
        started.append(copy)

    def arrived(dst, ssem, rsem, device):
        pltpu.make_async_remote_copy(
            src_ref=dst, dst_ref=dst, send_sem=ssem, recv_sem=rsem,
            device_id=device, device_id_type=pl.DeviceIdType.MESH,
        ).wait_recv()

    vel[pl.ds(96, 32), :] = jnp.zeros((32, 128), F32)
    loads[0].wait()
    for q in range(8):
        for base, comp, first, count in ((0, 0, 4 * q - 2, 9), (9, 1, 4 * q - 1, 7), (16, 2, 4 * q - 1, 7)):
            at = 0
            while at < count:
                plane = (first + at) % 32
                take = min(count - at, 32 - plane)
                pack[pl.ds(q * SLAB + base + at, take), :] = vel[pl.ds(comp * 32 + plane, take), :]
                at += take
    vel_t = vel[...].T
    vzpack[0] = vel_t[0:8]
    vzpack[1] = vel_t[120:128]
    loads[1].wait()
    for p in range(4):
        ypack[0, pl.ds(2 * p, 2), :] = theta[p, 0:2, :]
        ypack[1, pl.ds(2 * p, 2), :] = theta[p, 30:32, :]
    zpack[0] = theta[:, :, 0:128].reshape(128, 128).T[0:8]
    zpack[1] = theta[:, :, 128:256].reshape(128, 128).T[120:128]
    wown[...] = jnp.concatenate(
        [jnp.full((1, 128), weight[p], F32) for p in range(4)] + [jnp.zeros((4, 128), F32)], axis=0
    )

    def slot(b):
        return pl.ds(pl.multiple_of((b + 2) * SLAB, 8), SLAB)

    def part(first, offset, count):
        return pl.ds(pl.multiple_of(first + offset, 8), count)

    pl.semaphore_wait(barrier, len(peers))

    send(vzpack.at[1], vzrecv.at[0], v_send.at[0], v_recv.at[0], up_col)
    send(vzpack.at[0], vzrecv.at[1], v_send.at[1], v_recv.at[1], down_col)
    land = (blk + 2) * SLAB
    for n, q in enumerate(chips):
        send(
            pack.at[part(q * SLAB, 0, 16)], buf.at[part(land, 0, 16)],
            a_send.at[n], a_recv.at[n], {"blk": 2 * q + core},
        )
    send(theta.at[pl.ds(2, 2)], xlo, x_send.at[0], x_recv.at[0], up_blk)
    send(theta.at[pl.ds(0, 2)], xhi, x_send.at[1], x_recv.at[1], down_blk)
    send(wown, wlo, w_send.at[0], w_recv.at[0], up_blk)
    send(wown, whi, w_send.at[1], w_recv.at[1], down_blk)
    send(ypack.at[1], yrecv.at[0], y_send.at[0], y_recv.at[0], up_row)
    send(ypack.at[0], yrecv.at[1], y_send.at[1], y_recv.at[1], down_row)
    send(zpack.at[1], zrecv.at[pl.ds(0, 8)], z_send.at[0], z_recv.at[0], up_col)
    send(zpack.at[0], zrecv.at[pl.ds(8, 8)], z_send.at[1], z_recv.at[1], down_col)

    p_row, l_col = iota((128, 128), 0), iota((128, 128), 1)
    plane = p_row & 31
    comp = p_row >> 5
    place = jnp.where(comp == 0, plane & 15, jnp.where(comp == 1, 16 + (plane & 7), 24 + (plane & 7)))
    select = jnp.where((place == (l_col & 31)) & (comp < 3), 1.0, 0.0).astype(BF16)
    k_row, p_lane = iota((8, 128), 0), iota((8, 128), 1)
    plane8 = p_lane & 31
    inside0 = ((plane8 - 4 * k_row + 34) & 31) < 9
    inside1 = ((plane8 - 4 * k_row + 33) & 31) < 7
    lead = p_lane < 32
    window = (lead & inside0) | (jnp.logical_not(lead) & inside1)
    arrived(vzrecv.at[0], v_send.at[0], v_recv.at[0], down_col)
    arrived(vzrecv.at[1], v_send.at[1], v_recv.at[1], up_col)
    left, right = vzrecv[0], vzrecv[1]
    edges = jnp.concatenate(
        [
            jnp.where(window, jnp.broadcast_to(one, (8, 128)), 0.0)
            for one in (left[6:7], left[7:8], right[0:1], right[1:2])
        ],
        axis=0,
    )
    picked = sum(dot(piece, select) for piece in split3(edges))
    lane8 = iota((8, 128), 1) >> 5
    edge_rows = jnp.zeros((8, 128), F32)
    for e in range(4):
        edge_rows = jnp.where(lane8 == e, picked[8 * e : 8 * e + 8], edge_rows)
    for q in range(8):
        pack[pl.ds(q * SLAB + 23, 1), :] = edge_rows[q : q + 1]
    for n, q in enumerate(chips):
        send(
            pack.at[part(q * SLAB, 16, 8)], buf.at[part(land, 16, 8)],
            b_send.at[n], b_recv.at[n], {"blk": 2 * q + core},
        )
    own_slab = pl.ds(pl.multiple_of(chip * SLAB, 8), SLAB)
    send(pack.at[own_slab], buf.at[slot(blk)], p_send.at[7], p_recv.at[7], partner)
    buf[slot(blk), :] = pack[own_slab, :]

    for u in (2, 3, 4):
        loads[u].wait()
    loads[5].wait()
    kk, jj = iota((384, 256), 0), iota((384, 256), 1)
    at = jnp.where(kk < 256, kk, jnp.where(kk < 264, kk - 264, jnp.where(kk < 272, kk - 8, 4096)))
    stencil1, stencil2 = first_weights(at - jj), second_weights(at - jj)
    m1 = sum(dot(stencil1, piece, NT) for piece in split3(fz[...])) * (1.0 / 36.0)
    m1h[...], m1l[...] = split2(m1)
    m2 = sum(dot(stencil2, piece, NT) for piece in split3(sz[...])) * (1.0 / 44.0)
    m2h[...], m2l[...] = split2(m2)
    jy, ly = iota((32, 256), 0), iota((32, 256), 1)
    third = jnp.where(ly < 48, ly, jnp.where(ly < 96, ly - 48, jnp.where(ly < 144, ly - 96, 4096)))
    dy_ = third - 8 - jy
    my1 = sum(dot(piece, first_weights(dy_)) for piece in split3(fy[...])) * (1.0 / 36.0)
    my2 = sum(dot(piece, second_weights(dy_)) for piece in split3(sy[...])) * (1.0 / 44.0)
    both = jnp.concatenate([my1, my2], axis=0)
    high = both.astype(BF16).astype(F32)
    my[...] = jnp.where(iota((64, 256), 1) < 96, high, both - high).astype(BF16)
    kr, zr = iota((256, 384), 0), iota((256, 384), 1)
    group = (kr - 128) >> 5
    cell = jnp.where(kr < 128, kr, jnp.where(group < 2, group - 2, group + 126))
    zz = jnp.where(zr < 256, zr, jnp.where(zr < 264, zr - 264, jnp.where(zr < 272, zr - 8, 4096)))
    near = zz >> 1
    other = near + 2 * (zz & 1) - 1
    rz[...] = jnp.where(cell == near, 0.75, jnp.where(cell == other, 0.25, jnp.zeros((256, 384), F32))).astype(BF16)

    zrecv[pl.ds(16, 112), :] = jnp.zeros((112, 128), F32)
    for p in range(4):
        tpad[p, 0:8, :] = jnp.zeros((8, 256), F32)
        tpad[p, 40:48, :] = jnp.zeros((8, 256), F32)
        tpad[p, 8:40, :] = theta[p]
    arrived(zrecv.at[pl.ds(0, 8)], z_send.at[0], z_recv.at[0], down_col)
    arrived(zrecv.at[pl.ds(8, 8)], z_send.at[1], z_recv.at[1], up_col)
    side = zrecv[...].T
    th, tl = split2(theta[...].reshape(128, 256))
    sh, sl = split2(side)

    def along_z(mh, ml, ah, al, eh, el):
        h0, h1, l0, l1 = mh[0:256], mh[256:384], ml[0:256], ml[256:384]
        return dot(ah, h0) + dot(ah, l0) + dot(al, h0) + dot(eh, h1) + dot(eh, l1) + dot(el, h1)

    gz[...] = along_z(m1h[...], m1l[...], th, tl, sh, sl).reshape(4, 32, 256)
    lap[...] = along_z(m2h[...], m2l[...], th, tl, sh, sl).reshape(4, 32, 256)
    arrived(yrecv.at[0], y_send.at[0], y_recv.at[0], down_row)
    arrived(yrecv.at[1], y_send.at[1], y_recv.at[1], up_row)
    for p in range(4):
        tpad[p, 6:8, :] = yrecv[0, pl.ds(2 * p, 2), :]
        tpad[p, 40:42, :] = yrecv[1, pl.ds(2 * p, 2), :]
        ph, plow = split2(tpad[p])
        res = dot(my[:, 0:144], jnp.concatenate([ph, plow, ph], axis=0))
        gy[p] = res[0:32]
        lap[p] += res[32:64]

    for n, q in enumerate(senders):
        b = 2 * q + core
        first = (b + 2) * SLAB
        arrived(buf.at[part(first, 0, 16)], a_send.at[n], a_recv.at[n], {"blk": b})
        arrived(buf.at[part(first, 16, 8)], b_send.at[n], b_recv.at[n], {"blk": b})
        send(buf.at[slot(b)], buf.at[slot(b)], p_send.at[n], p_recv.at[n], partner)

    arrived(wlo, w_send.at[0], w_recv.at[0], down_blk)
    arrived(whi, w_send.at[1], w_recv.at[1], up_blk)
    s_row = iota((16, 128), 0)
    l_row = iota((1, 128), 1) & 31
    for t in range(8):
        low = lower[(4 * blk + t + 62) % 64]
        if t < 2:
            w = wlo[t + 2 : t + 3, :]
        elif t < 6:
            w = wown[t - 2 : t - 1, :]
        else:
            w = whi[t - 6 : t - 5, :]
        s0 = (low - 4 * chip + 34) & 31
        coef[t] = jnp.where(s_row == s0, 1.0 - w, jnp.where(s_row == s0 + 1, w, 0.0))
        for c in range(3):
            if c > 0 and not 2 <= t < 6:
                continue
            if c == 0:
                a0, a1 = low & 15, (low + 1) & 15
            else:
                a0, a1 = 8 + 8 * c + (low & 7), 8 + 8 * c + ((low + 1) & 7)
            line = 8 * c + t
            mix[pl.ds(line, 1), :] = jnp.where(l_row == a0, 1.0 - w, jnp.where(l_row == a1, w, 0.0))
    arrived(xlo, x_send.at[0], x_recv.at[0], down_blk)
    arrived(xhi, x_send.at[1], x_recv.at[1], up_blk)

    def tplane(t):
        if t < 2:
            return xlo[t]
        if t < 6:
            return theta[t - 2]
        return xhi[t - 6]

    for j in range(4):
        t = j + 2
        a, b_, c_, d_, m = tplane(t + 1), tplane(t - 1), tplane(t + 2), tplane(t - 2), tplane(t)
        one = 28.0 * (a - b_) + (c_ - d_)
        two = 48.0 * (a + b_) + 3.0 * (c_ + d_) - 102.0 * m
        for i in range(4):
            s1 = metric[i] * (fx[i, j] * (1.0 / 36.0))
            s2 = metric[i] * metric[i] * (sx[i, j] * (1.0 / 44.0))
            if j == 0:
                gx[i] = s1 * one
            else:
                gx[i] += s1 * one
            lap[i] += s2 * two

    for n, q in enumerate(senders):
        b = 2 * q + 1 - core
        arrived(buf.at[slot(b)], p_send.at[n], p_recv.at[n], partner)
    arrived(buf.at[slot(2 * chip + 1 - core)], p_send.at[7], p_recv.at[7], partner)
    send(buf.at[pl.ds(16 * SLAB, 2 * SLAB)], buf.at[pl.ds(0, 2 * SLAB)], r_send.at[0], r_recv.at[0], up_row)
    send(buf.at[pl.ds(2 * SLAB, 2 * SLAB)], buf.at[pl.ds(18 * SLAB, 2 * SLAB)], r_send.at[1], r_recv.at[1], down_row)
    buf[pl.ds(20 * SLAB, 4 * SLAB), :] = jnp.zeros((4 * SLAB, 128), F32)
    for p in range(4):
        fine1[p, 0:8, :] = jnp.zeros((8, 128), F32)
        fine1[p, 40:48, :] = jnp.zeros((8, 128), F32)
    efine[0:8, :] = jnp.zeros((8, 128), F32)
    efine[40:48, :] = jnp.zeros((8, 128), F32)
    arrived(buf.at[pl.ds(0, 2 * SLAB)], r_send.at[0], r_recv.at[0], down_row)
    arrived(buf.at[pl.ds(18 * SLAB, 2 * SLAB)], r_send.at[1], r_recv.at[1], up_row)

    def plane_of(line):
        return buf[pl.ds(line, 24, stride=SLAB), :]

    def refine_wide(value, target):
        vt[...] = value
        target[pl.ds(6, 18, stride=2), :] = 0.75 * vt[1:19] + 0.25 * vt[0:18]
        target[pl.ds(7, 18, stride=2), :] = 0.75 * vt[1:19] + 0.25 * vt[2:20]

    def refine_own(value, target):
        vt[...] = value
        target[pl.ds(0, 16, stride=2), :] = 0.75 * vt[2:18] + 0.25 * vt[1:17]
        target[pl.ds(1, 16, stride=2), :] = 0.75 * vt[2:18] + 0.25 * vt[3:19]

    refine_wide(plane_of(23), efine)
    edge_wide = efine[...]
    edge_own = efine[8:40, :]
    planes0 = [plane_of(s) for s in range(9)]
    for t in range(8):
        value = coef[t, 0:1, :] * planes0[0]
        for s in range(1, 9):
            value += coef[t, s : s + 1, :] * planes0[s]
        refine_own(value, fine0.at[t])
    for c, target, refine in ((1, fine1, refine_wide), (2, fine2, refine_own)):
        planes = [plane_of(2 + 7 * c + s) for s in range(7)]
        for p in range(4):
            value = coef[p + 2, 1:2, :] * planes[0]
            for s in range(1, 7):
                value += coef[p + 2, s + 1 : s + 2, :] * planes[s]
            refine(value, target.at[p])

    def wide(interior, edge, line, columns):
        rest = edge * mix[pl.ds(line, 1), :]
        ah, al = split2(jnp.concatenate([interior, rest], axis=1))
        matrix = rz[:, 0:columns]
        return dot(ah, matrix) + dot(al, matrix)

    flow_z = [wide(fine2[p], edge_own, 18 + p, 384) for p in range(4)]
    flow_z = jnp.concatenate(flow_z, axis=0)
    fh, fl = split2(flow_z[:, 0:256] * theta[...].reshape(128, 256))
    eh, el = split2(flow_z[:, 256:384] * zrecv[...].T)
    total = flow_z[:, 0:256] * gz[...].reshape(128, 256) + along_z(m1h[...], m1l[...], fh, fl, eh, el)
    out_ref[...] = 0.2 * lap[...] - 0.5 * total.reshape(4, 32, 256)
    for p in range(4):
        flow = wide(fine1[p], edge_wide, 10 + p, 256)
        ph, plow = split2(flow * tpad[p])
        slope = dot(my[0:32, 0:144], jnp.concatenate([ph, plow, ph], axis=0))
        own = flow[8:40]
        out_ref[p] -= 0.5 * (own * gy[p] + slope) + own
    flows = [wide(fine0[t], edge_own, t, 256) for t in range(8)]
    flux = [flows[t] * tplane(t) for t in range(8)]
    for i in range(4):
        out_ref[i] -= 0.5 * (flows[i + 2] * gx[i])
    for j in range(4):
        t = j + 2
        one = 28.0 * (flux[t + 1] - flux[t - 1]) + (flux[t + 2] - flux[t - 2])
        for i in range(4):
            out_ref[i] -= (0.5 * (metric[i] * (fx[i, j] * (1.0 / 36.0)))) * one

    for copy in started:
        copy.wait_send()


def local(theta, section, velocity, lower_plane, weight_x, metric_x,
          first_x, first_y, first_z, second_x, second_y, second_z):
    smem = pl.BlockSpec(memory_space=pltpu.SMEM)
    anywhere = pl.BlockSpec(memory_space=pl.ANY)

    def vm(*shape, kind=F32):
        return pltpu.VMEM(shape, kind)

    def sem(n):
        return pltpu.SemaphoreType.DMA((n,))

    tendency = pl.pallas_call(
        kernel,
        out_shape=jax.ShapeDtypeStruct((4, 32, 256), F32),
        in_specs=[smem] * 5 + [anywhere] * 6,
        out_specs=pl.BlockSpec(memory_space=pltpu.VMEM),
        scratch_shapes=[
            vm(4, 32, 256), vm(128, 128), vm(32, 32), vm(32, 32), vm(256, 256), vm(256, 256),
            vm(2, 32, 256), vm(2, 32, 256), vm(8, 128), vm(8, 128), vm(8, 128),
            vm(2, 8, 256), vm(2, 8, 256), vm(2, 8, 128), vm(128, 128), vm(2, 8, 128), vm(2, 8, 128),
            vm(8 * SLAB, 128), vm(24 * SLAB, 128), vm(8, 16, 128), vm(24, 128), vm(256, 384, kind=BF16),
            vm(384, 256, kind=BF16), vm(384, 256, kind=BF16), vm(384, 256, kind=BF16), vm(384, 256, kind=BF16),
            vm(64, 256, kind=BF16), vm(4, 48, 256), vm(24, 128),
            vm(8, 32, 128), vm(4, 48, 128), vm(4, 32, 128), vm(48, 128),
            vm(4, 32, 256), vm(4, 32, 256), vm(4, 32, 256), vm(4, 32, 256),
            sem(6), sem(2), sem(2), sem(2), sem(2), sem(2), sem(2), sem(2), sem(2), sem(2), sem(2),
            sem(7), sem(7), sem(7), sem(7), sem(8), sem(8), sem(2), sem(2),
        ],
        compiler_params=pltpu.CompilerParams(
            collective_id=0, has_side_effects=True, vmem_limit_bytes=32 * 1024 * 1024
        ),
    )(
        lower_plane, weight_x, metric_x, first_x, second_x,
        theta, velocity.reshape(96, 128), first_y, second_y, first_z, second_z,
    )
    section_new = (-5.0 / 9.0) * section + 0.2 * tendency
    theta_new = theta + (15.0 / 16.0) * section_new
    return (theta_new, section_new)


def solution(mesh):
    placed = (
        P("blk", "row", "col"),
        P("blk", "row", "col"),
        P(None, None, ("row", "blk"), "col"),
        P(),
        P("blk"),
        P("blk"),
        P(),
        P(),
        P(),
        P(),
        P(),
        P(),
    )
    return jax.shard_map(
        local,
        mesh=mesh,
        in_specs=placed,
        out_specs=(P("blk", "row", "col"), P("blk", "row", "col")),
        check_vma=False,
    )
```

```python
import jax
import jax.numpy as jnp
from jax import lax
from jax.experimental import pallas as pl
from jax.experimental.pallas import tpu as pltpu
from jax.sharding import PartitionSpec as P

F32 = jnp.float32
BF16 = jnp.bfloat16
SLAB = 24
NN = (((1,), (0,)), ((), ()))
NT = (((1,), (1,)), ((), ()))


def split2(x):
    high = x.astype(BF16)
    return high, (x - high.astype(F32)).astype(BF16)


def split3(x):
    high = x.astype(BF16)
    rest = x - high.astype(F32)
    mid = rest.astype(BF16)
    return high, mid, (rest - mid.astype(F32)).astype(BF16)


def dot(a, b, dims=NN):
    return lax.dot_general(a, b, dims, preferred_element_type=F32)


def iota(shape, dim):
    return lax.broadcasted_iota(jnp.int32, shape, dim)


def first_weights(d):
    zero = jnp.zeros(d.shape, F32)
    return jnp.where(
        d == 1, 28.0, jnp.where(d == -1, -28.0, jnp.where(d == 2, 1.0, jnp.where(d == -2, -1.0, zero)))
    ).astype(BF16)


def second_weights(d):
    zero = jnp.zeros(d.shape, F32)
    far = jnp.abs(d)
    return jnp.where(
        far == 0, -102.0, jnp.where(far == 1, 48.0, jnp.where(far == 2, 3.0, zero))
    ).astype(BF16)


def kernel(
    lower, weight, metric, fx, sx,
    theta_in, vel_in, fy_in, sy_in, fz_in, sz_in,
    out_ref,
    theta, vel, fy, sy, fz, sz,
    xlo, xhi, wown, wlo, whi, ypack, yrecv, zpack, zrecv, vzpack, vzrecv,
    pack, buf, coef, mix, rz, m1h, m1l, m2h, m2l, my, tpad, vt, fine0, fine1, fine2, efine,
    gx, gy, gz, lap,
    in_sem, x_send, x_recv, w_send, w_recv, y_send, y_recv, z_send, z_recv, v_send, v_recv,
    a_send, a_recv, p_send, p_recv, r_send, r_recv, h_send,
):
    row, col, blk = lax.axis_index("row"), lax.axis_index("col"), lax.axis_index("blk")
    rows, cols = lax.axis_size("row"), lax.axis_size("col")
    chip, core = blk // 2, blk % 2
    zhi, ypos = chip // 4, chip % 4

    loads = []
    for n, (src, dst) in enumerate(
        ((vel_in, vel.at[pl.ds(0, 96)]), (theta_in, theta), (fz_in, fz), (sz_in, sz), (fy_in, fy), (sy_in, sy))
    ):
        load = pltpu.make_async_copy(src, dst, in_sem.at[n])
        load.start()
        loads.append(load)

    partner = {"blk": 2 * chip + (1 - core)}
    up_blk, down_blk = {"blk": (blk + 1) % 16}, {"blk": (blk + 15) % 16}
    up_row, down_row = {"row": (row + 1) % rows}, {"row": (row + rows - 1) % rows}
    up_col, down_col = {"col": (col + 1) % cols}, {"col": (col + cols - 1) % cols}
    chips, senders = [], []
    for far, dy in ((1, 0), (1, 1), (1, 2), (1, 3), (0, 1), (0, 2), (0, 3)):
        chips.append(((zhi + far) % 2) * 4 + (ypos + dy) % 4)
        senders.append(((zhi + far) % 2) * 4 + (ypos + 4 - dy) % 4)

    barrier = pltpu.get_barrier_semaphore()
    outer = {"blk": (blk + 2 * core + 15) % 16}
    peers = [{"blk": 2 * q + core} for q in chips] + [partner, outer, up_col, down_col]
    peers += [up_row, down_row, {**up_row, **partner}, {**down_row, **partner}]
    for peer in peers:
        pl.semaphore_signal(barrier, inc=1, device_id=peer, device_id_type=pl.DeviceIdType.MESH)
    near_row = jnp.where(zhi == 0, up_row["row"], down_row["row"])
    edge_row = jnp.where(zhi == 0, down_row["row"], up_row["row"])
    at_edge = row == jnp.where(zhi == 0, 0, rows - 1)
    for n in (0, 1):
        owner = {"row": near_row, "blk": 14 * zhi + n}
        pl.semaphore_signal(barrier, inc=1, device_id=owner, device_id_type=pl.DeviceIdType.MESH)

    @pl.when(at_edge)
    def _():
        for n in (0, 1):
            owner = {"row": edge_row, "blk": 14 * (1 - zhi) + n}
            pl.semaphore_signal(barrier, inc=1, device_id=owner, device_id_type=pl.DeviceIdType.MESH)

    owns = (blk <= 1) | (blk >= 14)
    to_row = jnp.where(zhi == 0, down_row["row"], up_row["row"])
    owns_all = owns & (row == jnp.where(zhi == 0, 0, rows - 1))
    expected = len(peers) + jnp.where(owns, 8, 0) + jnp.where(owns_all, 8, 0)

    started = []

    def send(src, dst, ssem, rsem, device):
        copy = pltpu.make_async_remote_copy(
            src_ref=src, dst_ref=dst, send_sem=ssem, recv_sem=rsem,
            device_id=device, device_id_type=pl.DeviceIdType.MESH,
        )
        copy.start()
        started.append(copy)

    def arrived(dst, ssem, rsem, device):
        pltpu.make_async_remote_copy(
            src_ref=dst, dst_ref=dst, send_sem=ssem, recv_sem=rsem,
            device_id=device, device_id_type=pl.DeviceIdType.MESH,
        ).wait_recv()

    vel[pl.ds(96, 32), :] = jnp.zeros((32, 128), F32)
    loads[0].wait()
    vel_t = vel[...].T
    vzpack[0] = vel_t[0:8]
    vzpack[1] = vel_t[120:128]
    def slot(b):
        return pl.ds(pl.multiple_of((b + 2) * SLAB, 8), SLAB)

    def part(first, offset, count):
        return pl.ds(pl.multiple_of(first + offset, 8), count)

    pl.semaphore_wait(barrier, expected)

    send(vzpack.at[1], vzrecv.at[0], v_send.at[0], v_recv.at[0], up_col)
    send(vzpack.at[0], vzrecv.at[1], v_send.at[1], v_recv.at[1], down_col)
    for q in range(8):
        for base, comp, first, count in ((0, 0, 4 * q - 2, 9), (9, 1, 4 * q - 1, 7), (16, 2, 4 * q - 1, 7)):
            at = 0
            while at < count:
                plane = (first + at) % 32
                take = min(count - at, 32 - plane)
                pack[pl.ds(q * SLAB + base + at, take), :] = vel[pl.ds(comp * 32 + plane, take), :]
                at += take
    loads[1].wait()
    for p in range(4):
        ypack[0, pl.ds(2 * p, 2), :] = theta[p, 0:2, :]
        ypack[1, pl.ds(2 * p, 2), :] = theta[p, 30:32, :]
    send(ypack.at[1], yrecv.at[0], y_send.at[0], y_recv.at[0], up_row)
    send(ypack.at[0], yrecv.at[1], y_send.at[1], y_recv.at[1], down_row)
    send(theta.at[pl.ds(2, 2)], xlo, x_send.at[0], x_recv.at[0], up_blk)
    send(theta.at[pl.ds(0, 2)], xhi, x_send.at[1], x_recv.at[1], down_blk)
    wown[...] = jnp.concatenate(
        [jnp.full((1, 128), weight[p], F32) for p in range(4)] + [jnp.zeros((4, 128), F32)], axis=0
    )
    send(wown, wlo, w_send.at[0], w_recv.at[0], up_blk)
    send(wown, whi, w_send.at[1], w_recv.at[1], down_blk)
    zpack[0] = theta[:, :, 0:128].reshape(128, 128).T[0:8]
    zpack[1] = theta[:, :, 128:256].reshape(128, 128).T[120:128]
    send(zpack.at[1], zrecv.at[pl.ds(0, 8)], z_send.at[0], z_recv.at[0], up_col)
    send(zpack.at[0], zrecv.at[pl.ds(8, 8)], z_send.at[1], z_recv.at[1], down_col)

    p_row, l_col = iota((128, 128), 0), iota((128, 128), 1)
    plane = p_row & 31
    comp = p_row >> 5
    place = jnp.where(comp == 0, plane & 15, jnp.where(comp == 1, 16 + (plane & 7), 24 + (plane & 7)))
    select = jnp.where((place == (l_col & 31)) & (comp < 3), 1.0, 0.0).astype(BF16)
    k_row, p_lane = iota((8, 128), 0), iota((8, 128), 1)
    plane8 = p_lane & 31
    inside0 = ((plane8 - 4 * k_row + 34) & 31) < 9
    inside1 = ((plane8 - 4 * k_row + 33) & 31) < 7
    lead = p_lane < 32
    window = (lead & inside0) | (jnp.logical_not(lead) & inside1)
    arrived(vzrecv.at[0], v_send.at[0], v_recv.at[0], down_col)
    arrived(vzrecv.at[1], v_send.at[1], v_recv.at[1], up_col)
    left, right = vzrecv[0], vzrecv[1]
    edges = jnp.concatenate(
        [
            jnp.where(window, jnp.broadcast_to(one, (8, 128)), 0.0)
            for one in (left[6:7], left[7:8], right[0:1], right[1:2])
        ],
        axis=0,
    )
    picked = sum(dot(piece, select) for piece in split3(edges))
    lane8 = iota((8, 128), 1) >> 5
    edge_rows = jnp.zeros((8, 128), F32)
    for e in range(4):
        edge_rows = jnp.where(lane8 == e, picked[8 * e : 8 * e + 8], edge_rows)
    for q in range(8):
        pack[pl.ds(q * SLAB + 23, 1), :] = edge_rows[q : q + 1]
    own_slab = pl.ds(pl.multiple_of(chip * SLAB, 8), SLAB)

    def row_copies(src, side):
        device, place, which = ((up_row, core, core), (down_row, core + 18, core + 2))[side]
        return [
            pltpu.make_async_remote_copy(
                src_ref=src, dst_ref=buf.at[part(place * SLAB, 0, SLAB)],
                send_sem=r_send.at[2 * side + n], recv_sem=r_recv.at[which],
                device_id=where, device_id_type=pl.DeviceIdType.MESH,
            )
            for n, where in enumerate((device, {**device, **partner}))
        ]

    forward_up, forward_down = (zhi == 0) & (row < rows - 1), (zhi == 1) & (row > 0)

    def pass_on(src, q):
        @pl.when((q == 7) & forward_up)
        def _():
            for copy in row_copies(src, 0):
                copy.start()

        @pl.when((q == 0) & forward_down)
        def _():
            for copy in row_copies(src, 1):
                copy.start()

    def owner_copies(half):
        place = jnp.where(zhi == 0, 18, 0) + core
        copies = []
        for n in range(8):
            b = 8 * half + n
            copies.append(pltpu.make_async_remote_copy(
                src_ref=pack.at[part((b // 2) * SLAB, 0, SLAB)], dst_ref=buf.at[part(place * SLAB, 0, SLAB)],
                send_sem=h_send.at[b], recv_sem=r_recv.at[jnp.where(zhi == 0, 2, 0) + core],
                device_id={"row": to_row, "blk": b}, device_id_type=pl.DeviceIdType.MESH,
            ))
        return copies

    for n, q in enumerate(chips):
        send(
            pack.at[part(q * SLAB, 0, SLAB)], buf.at[slot(blk)], a_send.at[n], a_recv.at[n], {"blk": 2 * q + core}
        )
    @pl.when(owns)
    def _():
        for copy in owner_copies(zhi):
            copy.start()

    @pl.when(owns_all)
    def _():
        for copy in owner_copies(1 - zhi):
            copy.start()

    pass_on(pack.at[own_slab], chip)
    send(pack.at[own_slab], buf.at[slot(blk)], p_send.at[7], p_recv.at[7], partner)
    buf[slot(blk), :] = pack[own_slab, :]

    for u in (2, 3, 4):
        loads[u].wait()
    loads[5].wait()
    kk, jj = iota((384, 256), 0), iota((384, 256), 1)
    at = jnp.where(kk < 256, kk, jnp.where(kk < 264, kk - 264, jnp.where(kk < 272, kk - 8, 4096)))
    stencil1, stencil2 = first_weights(at - jj), second_weights(at - jj)
    m1 = sum(dot(stencil1, piece, NT) for piece in split3(fz[...])) * (1.0 / 36.0)
    m1h[...], m1l[...] = split2(m1)
    m2 = sum(dot(stencil2, piece, NT) for piece in split3(sz[...])) * (1.0 / 44.0)
    m2h[...], m2l[...] = split2(m2)
    jy, ly = iota((32, 256), 0), iota((32, 256), 1)
    third = jnp.where(ly < 48, ly, jnp.where(ly < 96, ly - 48, jnp.where(ly < 144, ly - 96, 4096)))
    dy_ = third - 8 - jy
    my1 = sum(dot(piece, first_weights(dy_)) for piece in split3(fy[...])) * (1.0 / 36.0)
    my2 = sum(dot(piece, second_weights(dy_)) for piece in split3(sy[...])) * (1.0 / 44.0)
    both = jnp.concatenate([my1, my2], axis=0)
    high = both.astype(BF16).astype(F32)
    my[...] = jnp.where(iota((64, 256), 1) < 96, high, both - high).astype(BF16)
    kr, zr = iota((256, 384), 0), iota((256, 384), 1)
    group = (kr - 128) >> 5
    cell = jnp.where(kr < 128, kr, jnp.where(group < 2, group - 2, group + 126))
    zz = jnp.where(zr < 256, zr, jnp.where(zr < 264, zr - 264, jnp.where(zr < 272, zr - 8, 4096)))
    near = zz >> 1
    other = near + 2 * (zz & 1) - 1
    rz[...] = jnp.where(cell == near, 0.75, jnp.where(cell == other, 0.25, jnp.zeros((256, 384), F32))).astype(BF16)

    zrecv[pl.ds(16, 112), :] = jnp.zeros((112, 128), F32)
    for p in range(4):
        tpad[p, 0:8, :] = jnp.zeros((8, 256), F32)
        tpad[p, 40:48, :] = jnp.zeros((8, 256), F32)
        tpad[p, 8:40, :] = theta[p]
    arrived(zrecv.at[pl.ds(0, 8)], z_send.at[0], z_recv.at[0], down_col)
    arrived(zrecv.at[pl.ds(8, 8)], z_send.at[1], z_recv.at[1], up_col)
    side = zrecv[...].T
    th, tl = split2(theta[...].reshape(128, 256))
    sh, sl = split2(side)

    def along_z(mh, ml, ah, al, eh, el):
        h0, h1, l0, l1 = mh[0:256], mh[256:384], ml[0:256], ml[256:384]
        return dot(ah, h0) + dot(ah, l0) + dot(al, h0) + dot(eh, h1) + dot(eh, l1) + dot(el, h1)

    gz[...] = along_z(m1h[...], m1l[...], th, tl, sh, sl).reshape(4, 32, 256)
    lap[...] = along_z(m2h[...], m2l[...], th, tl, sh, sl).reshape(4, 32, 256)
    arrived(yrecv.at[0], y_send.at[0], y_recv.at[0], down_row)
    arrived(yrecv.at[1], y_send.at[1], y_recv.at[1], up_row)
    for p in range(4):
        tpad[p, 6:8, :] = yrecv[0, pl.ds(2 * p, 2), :]
        tpad[p, 40:42, :] = yrecv[1, pl.ds(2 * p, 2), :]
        ph, plow = split2(tpad[p])
        res = dot(my[:, 0:144], jnp.concatenate([ph, plow, ph], axis=0))
        gy[p] = res[0:32]
        lap[p] += res[32:64]

    arrived(wlo, w_send.at[0], w_recv.at[0], down_blk)
    arrived(whi, w_send.at[1], w_recv.at[1], up_blk)
    s_row = iota((16, 128), 0)
    l_row = iota((1, 128), 1) & 31
    for t in range(8):
        low = lower[(4 * blk + t + 62) % 64]
        if t < 2:
            w = wlo[t + 2 : t + 3, :]
        elif t < 6:
            w = wown[t - 2 : t - 1, :]
        else:
            w = whi[t - 6 : t - 5, :]
        s0 = (low - 4 * chip + 34) & 31
        coef[t] = jnp.where(s_row == s0, 1.0 - w, jnp.where(s_row == s0 + 1, w, 0.0))
        for c in range(3):
            if c > 0 and not 2 <= t < 6:
                continue
            if c == 0:
                a0, a1 = low & 15, (low + 1) & 15
            else:
                a0, a1 = 8 + 8 * c + (low & 7), 8 + 8 * c + ((low + 1) & 7)
            line = 8 * c + t
            mix[pl.ds(line, 1), :] = jnp.where(l_row == a0, 1.0 - w, jnp.where(l_row == a1, w, 0.0))
    arrived(xlo, x_send.at[0], x_recv.at[0], down_blk)
    arrived(xhi, x_send.at[1], x_recv.at[1], up_blk)

    def tplane(t):
        if t < 2:
            return xlo[t]
        if t < 6:
            return theta[t - 2]
        return xhi[t - 6]

    for j in range(4):
        t = j + 2
        a, b_, c_, d_, m = tplane(t + 1), tplane(t - 1), tplane(t + 2), tplane(t - 2), tplane(t)
        one = 28.0 * (a - b_) + (c_ - d_)
        two = 48.0 * (a + b_) + 3.0 * (c_ + d_) - 102.0 * m
        for i in range(4):
            s1 = metric[i] * (fx[i, j] * (1.0 / 36.0))
            s2 = metric[i] * metric[i] * (sx[i, j] * (1.0 / 44.0))
            if j == 0:
                gx[i] = s1 * one
            else:
                gx[i] += s1 * one
            lap[i] += s2 * two

    buf[pl.ds(20 * SLAB, 4 * SLAB), :] = jnp.zeros((4 * SLAB, 128), F32)
    for p in range(4):
        fine1[p, 0:8, :] = jnp.zeros((8, 128), F32)
        fine1[p, 40:48, :] = jnp.zeros((8, 128), F32)
    efine[0:8, :] = jnp.zeros((8, 128), F32)
    efine[40:48, :] = jnp.zeros((8, 128), F32)
    for n in (4, 5, 6, 0, 1, 2, 3):
        b = 2 * senders[n] + core
        arrived(buf.at[slot(b)], a_send.at[n], a_recv.at[n], {"blk": b})
        pass_on(buf.at[slot(b)], senders[n])
        send(buf.at[slot(b)], buf.at[slot(b)], p_send.at[n], p_recv.at[n], partner)
    for n, q in enumerate(senders):
        arrived(buf.at[slot(2 * q + 1 - core)], p_send.at[n], p_recv.at[n], partner)
    arrived(buf.at[slot(2 * chip + 1 - core)], p_send.at[7], p_recv.at[7], partner)
    for n, place in enumerate((0, 1, 18, 19)):
        arrived(buf.at[pl.ds(place * SLAB, SLAB)], r_send.at[n], r_recv.at[n], up_row)

    def plane_of(line):
        return buf[pl.ds(line, 24, stride=SLAB), :]

    def refine_wide(value, target):
        vt[...] = value
        target[pl.ds(6, 18, stride=2), :] = 0.75 * vt[1:19] + 0.25 * vt[0:18]
        target[pl.ds(7, 18, stride=2), :] = 0.75 * vt[1:19] + 0.25 * vt[2:20]

    def refine_own(value, target):
        vt[...] = value
        target[pl.ds(0, 16, stride=2), :] = 0.75 * vt[2:18] + 0.25 * vt[1:17]
        target[pl.ds(1, 16, stride=2), :] = 0.75 * vt[2:18] + 0.25 * vt[3:19]

    refine_wide(plane_of(23), efine)
    edge_wide = efine[...]
    edge_own = efine[8:40, :]
    planes0 = [plane_of(s) for s in range(9)]
    for t in range(8):
        value = coef[t, 0:1, :] * planes0[0]
        for s in range(1, 9):
            value += coef[t, s : s + 1, :] * planes0[s]
        refine_own(value, fine0.at[t])
    for c, target, refine in ((1, fine1, refine_wide), (2, fine2, refine_own)):
        planes = [plane_of(2 + 7 * c + s) for s in range(7)]
        for p in range(4):
            value = coef[p + 2, 1:2, :] * planes[0]
            for s in range(1, 7):
                value += coef[p + 2, s + 1 : s + 2, :] * planes[s]
            refine(value, target.at[p])

    def wide(interior, edge, line, columns):
        rest = edge * mix[pl.ds(line, 1), :]
        ah, al = split2(jnp.concatenate([interior, rest], axis=1))
        matrix = rz[:, 0:columns]
        return dot(ah, matrix) + dot(al, matrix)

    flow_z = [wide(fine2[p], edge_own, 18 + p, 384) for p in range(4)]
    flow_z = jnp.concatenate(flow_z, axis=0)
    fh, fl = split2(flow_z[:, 0:256] * theta[...].reshape(128, 256))
    eh, el = split2(flow_z[:, 256:384] * zrecv[...].T)
    total = flow_z[:, 0:256] * gz[...].reshape(128, 256) + along_z(m1h[...], m1l[...], fh, fl, eh, el)
    out_ref[...] = 0.2 * lap[...] - 0.5 * total.reshape(4, 32, 256)
    for p in range(4):
        flow = wide(fine1[p], edge_wide, 10 + p, 256)
        ph, plow = split2(flow * tpad[p])
        slope = dot(my[0:32, 0:144], jnp.concatenate([ph, plow, ph], axis=0))
        own = flow[8:40]
        out_ref[p] -= 0.5 * (own * gy[p] + slope) + own
    flows = [wide(fine0[t], edge_own, t, 256) for t in range(8)]
    flux = [flows[t] * tplane(t) for t in range(8)]
    for i in range(4):
        out_ref[i] -= 0.5 * (flows[i + 2] * gx[i])
    for j in range(4):
        t = j + 2
        one = 28.0 * (flux[t + 1] - flux[t - 1]) + (flux[t + 2] - flux[t - 2])
        for i in range(4):
            out_ref[i] -= (0.5 * (metric[i] * (fx[i, j] * (1.0 / 36.0)))) * one

    for copy in started:
        copy.wait_send()

    for side, used in ((0, forward_up), (1, forward_down)):
        @pl.when(used)
        def _(side=side):
            for copy in row_copies(buf.at[pl.ds(0, SLAB)], side):
                copy.wait_send()

    @pl.when(owns)
    def _():
        for copy in owner_copies(zhi):
            copy.wait_send()

    @pl.when(owns_all)
    def _():
        for copy in owner_copies(1 - zhi):
            copy.wait_send()


def local(theta, section, velocity, lower_plane, weight_x, metric_x,
          first_x, first_y, first_z, second_x, second_y, second_z):
    smem = pl.BlockSpec(memory_space=pltpu.SMEM)
    anywhere = pl.BlockSpec(memory_space=pltpu.HBM)

    def vm(*shape, kind=F32):
        return pltpu.VMEM(shape, kind)

    def sem(n):
        return pltpu.SemaphoreType.DMA((n,))

    tendency = pl.pallas_call(
        kernel,
        out_shape=pltpu.VMEM((4, 32, 256), F32),
        in_specs=[smem] * 5 + [anywhere] * 6,
        out_specs=pl.BlockSpec(memory_space=pltpu.VMEM),
        scratch_shapes=[
            vm(4, 32, 256), vm(128, 128), vm(32, 32), vm(32, 32), vm(256, 256), vm(256, 256),
            vm(2, 32, 256), vm(2, 32, 256), vm(8, 128), vm(8, 128), vm(8, 128),
            vm(2, 8, 256), vm(2, 8, 256), vm(2, 8, 128), vm(128, 128), vm(2, 8, 128), vm(2, 8, 128),
            vm(8 * SLAB, 128), vm(24 * SLAB, 128), vm(8, 16, 128), vm(24, 128), vm(256, 384, kind=BF16),
            vm(384, 256, kind=BF16), vm(384, 256, kind=BF16), vm(384, 256, kind=BF16), vm(384, 256, kind=BF16),
            vm(64, 256, kind=BF16), vm(4, 48, 256), vm(24, 128),
            vm(8, 32, 128), vm(4, 48, 128), vm(4, 32, 128), vm(48, 128),
            vm(4, 32, 256), vm(4, 32, 256), vm(4, 32, 256), vm(4, 32, 256),
            sem(6), sem(2), sem(2), sem(2), sem(2), sem(2), sem(2), sem(2), sem(2), sem(2), sem(2),
            sem(7), sem(7), sem(8), sem(8), sem(4), sem(4), sem(16),
        ],
        compiler_params=pltpu.CompilerParams(
            collective_id=0, has_side_effects=True, vmem_limit_bytes=60 * 1024 * 1024
        ),
    )(
        lower_plane, weight_x, metric_x, first_x, second_x,
        theta, velocity.reshape(96, 128), first_y, second_y, first_z, second_z,
    )
    section_new = (-5.0 / 9.0) * section + 0.2 * tendency
    theta_new = theta + (15.0 / 16.0) * section_new
    return (theta_new, section_new)


def solution(mesh):
    placed = (
        P("blk", "row", "col"),
        P("blk", "row", "col"),
        P(None, None, ("row", "blk"), "col"),
        P(),
        P("blk"),
        P("blk"),
        P(),
        P(),
        P(),
        P(),
        P(),
        P(),
    )
    return jax.shard_map(
        local,
        mesh=mesh,
        in_specs=placed,
        out_specs=(P("blk", "row", "col"), P("blk", "row", "col")),
        check_vma=False,
    )
```

```python
import jax
import jax.numpy as jnp
from jax import lax
from jax.experimental import pallas as pl
from jax.experimental.pallas import tpu as pltpu
from jax.sharding import PartitionSpec as P

F32 = jnp.float32
BF16 = jnp.bfloat16
SLAB = 24
NN = (((1,), (0,)), ((), ()))
NT = (((1,), (1,)), ((), ()))


def split2(x):
    high = x.astype(BF16)
    return high, (x - high.astype(F32)).astype(BF16)


def split3(x):
    high = x.astype(BF16)
    rest = x - high.astype(F32)
    mid = rest.astype(BF16)
    return high, mid, (rest - mid.astype(F32)).astype(BF16)


def dot(a, b, dims=NN):
    return lax.dot_general(a, b, dims, preferred_element_type=F32)


def iota(shape, dim):
    return lax.broadcasted_iota(jnp.int32, shape, dim)


def first_weights(d):
    zero = jnp.zeros(d.shape, F32)
    return jnp.where(
        d == 1, 28.0, jnp.where(d == -1, -28.0, jnp.where(d == 2, 1.0, jnp.where(d == -2, -1.0, zero)))
    ).astype(BF16)


def second_weights(d):
    zero = jnp.zeros(d.shape, F32)
    far = jnp.abs(d)
    return jnp.where(
        far == 0, -102.0, jnp.where(far == 1, 48.0, jnp.where(far == 2, 3.0, zero))
    ).astype(BF16)


def kernel(
    lower, weight, metric, fx, sx,
    theta_in, vel_in, fy_in, sy_in, fz_in, sz_in,
    out_ref,
    theta, vel, fy, sy, fz, sz,
    xlo, xhi, wown, wlo, whi, ypack, yrecv, zpack, zrecv, vzpack, vzrecv,
    pack, buf, coef, mix, rz, m1h, m1l, m2h, m2l, my, tpad, vt, fine0, fine1, fine2, efine,
    gx, gy, gz, lap,
    in_sem, x_send, x_recv, w_send, w_recv, y_send, y_recv, z_send, z_recv, v_send, v_recv,
    a_send, a_recv, p_send, p_recv, r_send, r_recv, h_send,
):
    row, col, blk = lax.axis_index("row"), lax.axis_index("col"), lax.axis_index("blk")
    rows, cols = lax.axis_size("row"), lax.axis_size("col")
    chip, core = blk // 2, blk % 2
    zhi, ypos = chip // 4, chip % 4

    loads = []
    for n, (src, dst) in enumerate(
        ((vel_in, vel.at[pl.ds(0, 96)]), (theta_in, theta), (fz_in, fz), (sz_in, sz), (fy_in, fy), (sy_in, sy))
    ):
        load = pltpu.make_async_copy(src, dst, in_sem.at[n])
        load.start()
        loads.append(load)

    partner = {"blk": 2 * chip + (1 - core)}
    up_blk, down_blk = {"blk": (blk + 1) % 16}, {"blk": (blk + 15) % 16}
    up_row, down_row = {"row": (row + 1) % rows}, {"row": (row + rows - 1) % rows}
    up_col, down_col = {"col": (col + 1) % cols}, {"col": (col + cols - 1) % cols}
    chips, senders = [], []
    for far, dy in ((1, 0), (1, 1), (1, 2), (1, 3), (0, 1), (0, 2), (0, 3)):
        chips.append(((zhi + far) % 2) * 4 + (ypos + dy) % 4)
        senders.append(((zhi + far) % 2) * 4 + (ypos + 4 - dy) % 4)

    barrier = pltpu.get_barrier_semaphore()
    outer = {"blk": (blk + 2 * core + 15) % 16}
    peers = [{"blk": 2 * q + core} for q in chips] + [partner, outer, up_col, down_col]
    peers += [up_row, down_row, {**up_row, **partner}, {**down_row, **partner}]
    for peer in peers:
        pl.semaphore_signal(barrier, inc=1, device_id=peer, device_id_type=pl.DeviceIdType.MESH)
    near_row = jnp.where(zhi == 0, up_row["row"], down_row["row"])
    edge_row = jnp.where(zhi == 0, down_row["row"], up_row["row"])
    at_edge = row == jnp.where(zhi == 0, 0, rows - 1)
    for n in (0, 1):
        owner = {"row": near_row, "blk": 14 * zhi + n}
        pl.semaphore_signal(barrier, inc=1, device_id=owner, device_id_type=pl.DeviceIdType.MESH)

    @pl.when(at_edge)
    def _():
        for n in (0, 1):
            owner = {"row": edge_row, "blk": 14 * (1 - zhi) + n}
            pl.semaphore_signal(barrier, inc=1, device_id=owner, device_id_type=pl.DeviceIdType.MESH)

    owns = (blk <= 1) | (blk >= 14)
    to_row = jnp.where(zhi == 0, down_row["row"], up_row["row"])
    owns_all = owns & (row == jnp.where(zhi == 0, 0, rows - 1))
    expected = len(peers) + jnp.where(owns, 8, 0) + jnp.where(owns_all, 8, 0)

    started = []

    def send(src, dst, ssem, rsem, device):
        copy = pltpu.make_async_remote_copy(
            src_ref=src, dst_ref=dst, send_sem=ssem, recv_sem=rsem,
            device_id=device, device_id_type=pl.DeviceIdType.MESH,
        )
        copy.start()
        started.append(copy)

    def arrived(dst, ssem, rsem, device):
        pltpu.make_async_remote_copy(
            src_ref=dst, dst_ref=dst, send_sem=ssem, recv_sem=rsem,
            device_id=device, device_id_type=pl.DeviceIdType.MESH,
        ).wait_recv()

    vel[pl.ds(96, 32), :] = jnp.zeros((32, 128), F32)
    loads[0].wait()
    vel_t = vel[...].T
    p_row, l_col = iota((128, 128), 0), iota((128, 128), 1)
    plane = p_row & 31
    comp = p_row >> 5
    place = jnp.where(comp == 0, plane & 15, jnp.where(comp == 1, 16 + (plane & 7), 24 + (plane & 7)))
    select = jnp.where((place == (l_col & 31)) & (comp < 3), 1.0, 0.0).astype(BF16)
    k_row, p_lane = iota((8, 128), 0), iota((8, 128), 1)
    plane8 = p_lane & 31
    inside0 = ((plane8 - 4 * k_row + 34) & 31) < 9
    inside1 = ((plane8 - 4 * k_row + 33) & 31) < 7
    lead = p_lane < 32
    window = (lead & inside0) | (jnp.logical_not(lead) & inside1)
    edges = jnp.concatenate(
        [jnp.where(window, jnp.broadcast_to(vel_t[e : e + 1], (8, 128)), 0.0) for e in (0, 1, 126, 127)], axis=0
    )
    picked = sum(dot(piece, select) for piece in split3(edges))
    lane8 = iota((8, 128), 1) >> 5
    nothing = jnp.zeros((8, 128), F32)
    vzpack[0] = jnp.where(lane8 == 2, picked[0:8], jnp.where(lane8 == 3, picked[8:16], nothing))
    vzpack[1] = jnp.where(lane8 == 0, picked[16:24], jnp.where(lane8 == 1, picked[24:32], nothing))
    for q in range(8):
        for base, comp, first, count in ((0, 0, 4 * q - 2, 9), (9, 1, 4 * q - 1, 7), (16, 2, 4 * q - 1, 7)):
            at = 0
            while at < count:
                plane = (first + at) % 32
                take = min(count - at, 32 - plane)
                pack[pl.ds(q * SLAB + base + at, take), :] = vel[pl.ds(comp * 32 + plane, take), :]
                at += take
    loads[1].wait()
    for p in range(4):
        ypack[0, pl.ds(2 * p, 2), :] = theta[p, 0:2, :]
        ypack[1, pl.ds(2 * p, 2), :] = theta[p, 30:32, :]

    def slot(b):
        return pl.ds(pl.multiple_of((b + 2) * SLAB, 8), SLAB)

    def part(first, offset, count):
        return pl.ds(pl.multiple_of(first + offset, 8), count)

    pl.semaphore_wait(barrier, expected)

    send(vzpack.at[1], vzrecv.at[0], v_send.at[0], v_recv.at[0], up_col)
    send(vzpack.at[0], vzrecv.at[1], v_send.at[1], v_recv.at[1], down_col)
    send(ypack.at[1], yrecv.at[0], y_send.at[0], y_recv.at[0], up_row)
    send(ypack.at[0], yrecv.at[1], y_send.at[1], y_recv.at[1], down_row)
    send(theta.at[pl.ds(2, 2)], xlo, x_send.at[0], x_recv.at[0], up_blk)
    send(theta.at[pl.ds(0, 2)], xhi, x_send.at[1], x_recv.at[1], down_blk)
    wown[...] = jnp.concatenate(
        [jnp.full((1, 128), weight[p], F32) for p in range(4)] + [jnp.zeros((4, 128), F32)], axis=0
    )
    send(wown, wlo, w_send.at[0], w_recv.at[0], up_blk)
    send(wown, whi, w_send.at[1], w_recv.at[1], down_blk)
    zpack[0] = theta[:, :, 0:128].reshape(128, 128).T[0:8]
    zpack[1] = theta[:, :, 128:256].reshape(128, 128).T[120:128]
    send(zpack.at[1], zrecv.at[pl.ds(0, 8)], z_send.at[0], z_recv.at[0], up_col)
    send(zpack.at[0], zrecv.at[pl.ds(8, 8)], z_send.at[1], z_recv.at[1], down_col)

    arrived(vzrecv.at[0], v_send.at[0], v_recv.at[0], down_col)
    arrived(vzrecv.at[1], v_send.at[1], v_recv.at[1], up_col)
    edge_rows = vzrecv[0] + vzrecv[1]
    for q in range(8):
        pack[pl.ds(q * SLAB + 23, 1), :] = edge_rows[q : q + 1]

    own_slab = pl.ds(pl.multiple_of(chip * SLAB, 8), SLAB)

    def row_copies(src, side):
        device, place, which = ((up_row, core, core), (down_row, core + 18, core + 2))[side]
        return [
            pltpu.make_async_remote_copy(
                src_ref=src, dst_ref=buf.at[part(place * SLAB, 0, SLAB)],
                send_sem=r_send.at[2 * side + n], recv_sem=r_recv.at[which],
                device_id=where, device_id_type=pl.DeviceIdType.MESH,
            )
            for n, where in enumerate((device, {**device, **partner}))
        ]

    forward_up, forward_down = (zhi == 0) & (row < rows - 1), (zhi == 1) & (row > 0)

    def pass_on(src, q):
        @pl.when((q == 7) & forward_up)
        def _():
            for copy in row_copies(src, 0):
                copy.start()

        @pl.when((q == 0) & forward_down)
        def _():
            for copy in row_copies(src, 1):
                copy.start()

    def owner_copies(half):
        place = jnp.where(zhi == 0, 18, 0) + core
        copies = []
        for n in range(8):
            b = 8 * half + n
            copies.append(pltpu.make_async_remote_copy(
                src_ref=pack.at[part((b // 2) * SLAB, 0, SLAB)], dst_ref=buf.at[part(place * SLAB, 0, SLAB)],
                send_sem=h_send.at[b], recv_sem=r_recv.at[jnp.where(zhi == 0, 2, 0) + core],
                device_id={"row": to_row, "blk": b}, device_id_type=pl.DeviceIdType.MESH,
            ))
        return copies

    for n, q in enumerate(chips):
        send(
            pack.at[part(q * SLAB, 0, SLAB)], buf.at[slot(blk)], a_send.at[n], a_recv.at[n], {"blk": 2 * q + core}
        )
    @pl.when(owns)
    def _():
        for copy in owner_copies(zhi):
            copy.start()

    @pl.when(owns_all)
    def _():
        for copy in owner_copies(1 - zhi):
            copy.start()

    pass_on(pack.at[own_slab], chip)
    send(pack.at[own_slab], buf.at[slot(blk)], p_send.at[7], p_recv.at[7], partner)
    buf[slot(blk), :] = pack[own_slab, :]

    for u in (2, 3, 4):
        loads[u].wait()
    loads[5].wait()
    kk, jj = iota((384, 256), 0), iota((384, 256), 1)
    at = jnp.where(kk < 256, kk, jnp.where(kk < 264, kk - 264, jnp.where(kk < 272, kk - 8, 4096)))
    stencil1, stencil2 = first_weights(at - jj), second_weights(at - jj)
    m1 = sum(dot(stencil1, piece, NT) for piece in split3(fz[...])) * (1.0 / 36.0)
    m1h[...], m1l[...] = split2(m1)
    m2 = sum(dot(stencil2, piece, NT) for piece in split3(sz[...])) * (1.0 / 44.0)
    m2h[...], m2l[...] = split2(m2)
    jy, ly = iota((32, 256), 0), iota((32, 256), 1)
    third = jnp.where(ly < 48, ly, jnp.where(ly < 96, ly - 48, jnp.where(ly < 144, ly - 96, 4096)))
    dy_ = third - 8 - jy
    my1 = sum(dot(piece, first_weights(dy_)) for piece in split3(fy[...])) * (1.0 / 36.0)
    my2 = sum(dot(piece, second_weights(dy_)) for piece in split3(sy[...])) * (1.0 / 44.0)
    both = jnp.concatenate([my1, my2], axis=0)
    high = both.astype(BF16).astype(F32)
    my[...] = jnp.where(iota((64, 256), 1) < 96, high, both - high).astype(BF16)
    kr, zr = iota((256, 384), 0), iota((256, 384), 1)
    group = (kr - 128) >> 5
    cell = jnp.where(kr < 128, kr, jnp.where(group < 2, group - 2, group + 126))
    zz = jnp.where(zr < 256, zr, jnp.where(zr < 264, zr - 264, jnp.where(zr < 272, zr - 8, 4096)))
    near = zz >> 1
    other = near + 2 * (zz & 1) - 1
    rz[...] = jnp.where(cell == near, 0.75, jnp.where(cell == other, 0.25, jnp.zeros((256, 384), F32))).astype(BF16)

    zrecv[pl.ds(16, 112), :] = jnp.zeros((112, 128), F32)
    for p in range(4):
        tpad[p, 0:8, :] = jnp.zeros((8, 256), F32)
        tpad[p, 40:48, :] = jnp.zeros((8, 256), F32)
        tpad[p, 8:40, :] = theta[p]
    arrived(zrecv.at[pl.ds(0, 8)], z_send.at[0], z_recv.at[0], down_col)
    arrived(zrecv.at[pl.ds(8, 8)], z_send.at[1], z_recv.at[1], up_col)
    side = zrecv[...].T
    th, tl = split2(theta[...].reshape(128, 256))
    sh, sl = split2(side)

    def along_z(mh, ml, ah, al, eh, el):
        h0, h1, l0, l1 = mh[0:256], mh[256:384], ml[0:256], ml[256:384]
        return dot(ah, h0) + dot(ah, l0) + dot(al, h0) + dot(eh, h1) + dot(eh, l1) + dot(el, h1)

    gz[...] = along_z(m1h[...], m1l[...], th, tl, sh, sl).reshape(4, 32, 256)
    lap[...] = along_z(m2h[...], m2l[...], th, tl, sh, sl).reshape(4, 32, 256)
    arrived(yrecv.at[0], y_send.at[0], y_recv.at[0], down_row)
    arrived(yrecv.at[1], y_send.at[1], y_recv.at[1], up_row)
    for p in range(4):
        tpad[p, 6:8, :] = yrecv[0, pl.ds(2 * p, 2), :]
        tpad[p, 40:42, :] = yrecv[1, pl.ds(2 * p, 2), :]
        ph, plow = split2(tpad[p])
        res = dot(my[:, 0:144], jnp.concatenate([ph, plow, ph], axis=0))
        gy[p] = res[0:32]
        lap[p] += res[32:64]

    for n in (4, 5, 6, 0, 1, 2, 3):
        b = 2 * senders[n] + core
        arrived(buf.at[slot(b)], a_send.at[n], a_recv.at[n], {"blk": b})
        pass_on(buf.at[slot(b)], senders[n])
        send(buf.at[slot(b)], buf.at[slot(b)], p_send.at[n], p_recv.at[n], partner)
    arrived(wlo, w_send.at[0], w_recv.at[0], down_blk)
    arrived(whi, w_send.at[1], w_recv.at[1], up_blk)
    s_row = iota((16, 128), 0)
    l_row = iota((1, 128), 1) & 31
    for t in range(8):
        low = lower[(4 * blk + t + 62) % 64]
        if t < 2:
            w = wlo[t + 2 : t + 3, :]
        elif t < 6:
            w = wown[t - 2 : t - 1, :]
        else:
            w = whi[t - 6 : t - 5, :]
        s0 = (low - 4 * chip + 34) & 31
        coef[t] = jnp.where(s_row == s0, 1.0 - w, jnp.where(s_row == s0 + 1, w, 0.0))
        for c in range(3):
            if c > 0 and not 2 <= t < 6:
                continue
            if c == 0:
                a0, a1 = low & 15, (low + 1) & 15
            else:
                a0, a1 = 8 + 8 * c + (low & 7), 8 + 8 * c + ((low + 1) & 7)
            line = 8 * c + t
            mix[pl.ds(line, 1), :] = jnp.where(l_row == a0, 1.0 - w, jnp.where(l_row == a1, w, 0.0))
    arrived(xlo, x_send.at[0], x_recv.at[0], down_blk)
    arrived(xhi, x_send.at[1], x_recv.at[1], up_blk)

    def tplane(t):
        if t < 2:
            return xlo[t]
        if t < 6:
            return theta[t - 2]
        return xhi[t - 6]

    for j in range(4):
        t = j + 2
        a, b_, c_, d_, m = tplane(t + 1), tplane(t - 1), tplane(t + 2), tplane(t - 2), tplane(t)
        one = 28.0 * (a - b_) + (c_ - d_)
        two = 48.0 * (a + b_) + 3.0 * (c_ + d_) - 102.0 * m
        for i in range(4):
            s1 = metric[i] * (fx[i, j] * (1.0 / 36.0))
            s2 = metric[i] * metric[i] * (sx[i, j] * (1.0 / 44.0))
            if j == 0:
                gx[i] = s1 * one
            else:
                gx[i] += s1 * one
            lap[i] += s2 * two

    buf[pl.ds(20 * SLAB, 4 * SLAB), :] = jnp.zeros((4 * SLAB, 128), F32)
    for p in range(4):
        fine1[p, 0:8, :] = jnp.zeros((8, 128), F32)
        fine1[p, 40:48, :] = jnp.zeros((8, 128), F32)
    efine[0:8, :] = jnp.zeros((8, 128), F32)
    efine[40:48, :] = jnp.zeros((8, 128), F32)
    for n, q in enumerate(senders):
        arrived(buf.at[slot(2 * q + 1 - core)], p_send.at[n], p_recv.at[n], partner)
    arrived(buf.at[slot(2 * chip + 1 - core)], p_send.at[7], p_recv.at[7], partner)
    for n, place in enumerate((0, 1, 18, 19)):
        arrived(buf.at[pl.ds(place * SLAB, SLAB)], r_send.at[n], r_recv.at[n], up_row)

    def plane_of(line):
        return buf[pl.ds(line, 24, stride=SLAB), :]

    def refine_wide(value, target):
        vt[...] = value
        target[pl.ds(6, 18, stride=2), :] = 0.75 * vt[1:19] + 0.25 * vt[0:18]
        target[pl.ds(7, 18, stride=2), :] = 0.75 * vt[1:19] + 0.25 * vt[2:20]

    def refine_own(value, target):
        vt[...] = value
        target[pl.ds(0, 16, stride=2), :] = 0.75 * vt[2:18] + 0.25 * vt[1:17]
        target[pl.ds(1, 16, stride=2), :] = 0.75 * vt[2:18] + 0.25 * vt[3:19]

    refine_wide(plane_of(23), efine)
    edge_wide = efine[...]
    edge_own = efine[8:40, :]
    planes0 = [plane_of(s) for s in range(9)]
    for t in range(8):
        value = coef[t, 0:1, :] * planes0[0]
        for s in range(1, 9):
            value += coef[t, s : s + 1, :] * planes0[s]
        refine_own(value, fine0.at[t])
    for c, target, refine in ((1, fine1, refine_wide), (2, fine2, refine_own)):
        planes = [plane_of(2 + 7 * c + s) for s in range(7)]
        for p in range(4):
            value = coef[p + 2, 1:2, :] * planes[0]
            for s in range(1, 7):
                value += coef[p + 2, s + 1 : s + 2, :] * planes[s]
            refine(value, target.at[p])

    lines = [(fine2[p], edge_own, 18 + p) for p in range(4)]
    lines += [(fine1[p], edge_wide, 10 + p) for p in range(4)]
    lines += [(fine0[t], edge_own, t) for t in range(8)]
    interior = jnp.concatenate([one for one, _, _ in lines], axis=0)
    sides = jnp.concatenate([edge * mix[pl.ds(line, 1), :] for _, edge, line in lines], axis=0)
    xh, xl = split2(jnp.concatenate([interior, sides], axis=1))
    flow = dot(xh, rz[:, 0:256]) + dot(xl, rz[:, 0:256])
    flow_side = dot(xh[0:128], rz[:, 256:384]) + dot(xl[0:128], rz[:, 256:384])

    fh, fl = split2(flow[0:128] * theta[...].reshape(128, 256))
    eh, el = split2(flow_side * zrecv[...].T)
    total = flow[0:128] * gz[...].reshape(128, 256) + along_z(m1h[...], m1l[...], fh, fl, eh, el)
    out_ref[...] = 0.2 * lap[...] - 0.5 * total.reshape(4, 32, 256)
    for p in range(4):
        flow_y = flow[128 + 48 * p : 176 + 48 * p]
        ph, plow = split2(flow_y * tpad[p])
        slope = dot(my[0:32, 0:144], jnp.concatenate([ph, plow, ph], axis=0))
        own = flow_y[8:40]
        out_ref[p] -= 0.5 * (own * gy[p] + slope) + own
    flows = [flow[320 + 32 * t : 352 + 32 * t] for t in range(8)]
    flux = [flows[t] * tplane(t) for t in range(8)]
    for i in range(4):
        out_ref[i] -= 0.5 * (flows[i + 2] * gx[i])
    for j in range(4):
        t = j + 2
        one = 28.0 * (flux[t + 1] - flux[t - 1]) + (flux[t + 2] - flux[t - 2])
        for i in range(4):
            out_ref[i] -= (0.5 * (metric[i] * (fx[i, j] * (1.0 / 36.0)))) * one

    for copy in started:
        copy.wait_send()

    for side, used in ((0, forward_up), (1, forward_down)):
        @pl.when(used)
        def _(side=side):
            for copy in row_copies(buf.at[pl.ds(0, SLAB)], side):
                copy.wait_send()

    @pl.when(owns)
    def _():
        for copy in owner_copies(zhi):
            copy.wait_send()

    @pl.when(owns_all)
    def _():
        for copy in owner_copies(1 - zhi):
            copy.wait_send()


def local(theta, section, velocity, lower_plane, weight_x, metric_x,
          first_x, first_y, first_z, second_x, second_y, second_z):
    smem = pl.BlockSpec(memory_space=pltpu.SMEM)
    anywhere = pl.BlockSpec(memory_space=pltpu.HBM)

    def vm(*shape, kind=F32):
        return pltpu.VMEM(shape, kind)

    def sem(n):
        return pltpu.SemaphoreType.DMA((n,))

    tendency = pl.pallas_call(
        kernel,
        out_shape=pltpu.VMEM((4, 32, 256), F32),
        in_specs=[smem] * 5 + [anywhere] * 6,
        out_specs=pl.BlockSpec(memory_space=pltpu.VMEM),
        scratch_shapes=[
            vm(4, 32, 256), vm(128, 128), vm(32, 32), vm(32, 32), vm(256, 256), vm(256, 256),
            vm(2, 32, 256), vm(2, 32, 256), vm(8, 128), vm(8, 128), vm(8, 128),
            vm(2, 8, 256), vm(2, 8, 256), vm(2, 8, 128), vm(128, 128), vm(2, 8, 128), vm(2, 8, 128),
            vm(8 * SLAB, 128), vm(24 * SLAB, 128), vm(8, 16, 128), vm(24, 128), vm(256, 384, kind=BF16),
            vm(384, 256, kind=BF16), vm(384, 256, kind=BF16), vm(384, 256, kind=BF16), vm(384, 256, kind=BF16),
            vm(64, 256, kind=BF16), vm(4, 48, 256), vm(24, 128),
            vm(8, 32, 128), vm(4, 48, 128), vm(4, 32, 128), vm(48, 128),
            vm(4, 32, 256), vm(4, 32, 256), vm(4, 32, 256), vm(4, 32, 256),
            sem(6), sem(2), sem(2), sem(2), sem(2), sem(2), sem(2), sem(2), sem(2), sem(2), sem(2),
            sem(7), sem(7), sem(8), sem(8), sem(4), sem(4), sem(16),
        ],
        compiler_params=pltpu.CompilerParams(
            collective_id=0, has_side_effects=True, vmem_limit_bytes=60 * 1024 * 1024
        ),
    )(
        lower_plane, weight_x, metric_x, first_x, second_x,
        theta, velocity.reshape(96, 128), first_y, second_y, first_z, second_z,
    )
    section_new = (-5.0 / 9.0) * section + 0.2 * tendency
    theta_new = theta + (15.0 / 16.0) * section_new
    return (theta_new, section_new)


def solution(mesh):
    placed = (
        P("blk", "row", "col"),
        P("blk", "row", "col"),
        P(None, None, ("row", "blk"), "col"),
        P(),
        P("blk"),
        P("blk"),
        P(),
        P(),
        P(),
        P(),
        P(),
        P(),
    )
    return jax.shard_map(
        local,
        mesh=mesh,
        in_specs=placed,
        out_specs=(P("blk", "row", "col"), P("blk", "row", "col")),
        check_vma=False,
    )
```

```python
import jax
import jax.numpy as jnp
from jax import lax
from jax.experimental import pallas as pl
from jax.experimental.pallas import tpu as pltpu
from jax.sharding import PartitionSpec as P

F32 = jnp.float32
BF16 = jnp.bfloat16
SLAB = 24
NN = (((1,), (0,)), ((), ()))
NT = (((1,), (1,)), ((), ()))


def split2(x):
    high = x.astype(BF16)
    return high, (x - high.astype(F32)).astype(BF16)


def split3(x):
    high = x.astype(BF16)
    rest = x - high.astype(F32)
    mid = rest.astype(BF16)
    return high, mid, (rest - mid.astype(F32)).astype(BF16)


def dot(a, b, dims=NN):
    return lax.dot_general(a, b, dims, preferred_element_type=F32)


def iota(shape, dim):
    return lax.broadcasted_iota(jnp.int32, shape, dim)


def first_weights(d):
    zero = jnp.zeros(d.shape, F32)
    return jnp.where(
        d == 1, 28.0, jnp.where(d == -1, -28.0, jnp.where(d == 2, 1.0, jnp.where(d == -2, -1.0, zero)))
    ).astype(BF16)


def second_weights(d):
    zero = jnp.zeros(d.shape, F32)
    far = jnp.abs(d)
    return jnp.where(
        far == 0, -102.0, jnp.where(far == 1, 48.0, jnp.where(far == 2, 3.0, zero))
    ).astype(BF16)


def kernel(
    lower, weight, metric, fx, sx,
    theta_in, vel_in, fy_in, sy_in, fz_in, sz_in,
    out_ref,
    theta, vel, fy, sy, fz, sz,
    xlo, xhi, wown, wlo, whi, ypack, yrecv, zpack, zrecv, vzpack, vzrecv,
    pack, buf, coef, mix, rz, m1h, m1l, m2h, m2l, my, tpad, vt, fine0, fine1, fine2, efine,
    gx, gy, gz, lap,
    in_sem, x_send, x_recv, w_send, w_recv, y_send, y_recv, z_send, z_recv, v_send, v_recv,
    a_send, a_recv, p_send, p_recv, r_send, r_recv, h_send,
):
    row, col, blk = lax.axis_index("row"), lax.axis_index("col"), lax.axis_index("blk")
    rows, cols = lax.axis_size("row"), lax.axis_size("col")
    chip, core = blk // 2, blk % 2
    zhi, ypos = chip // 4, chip % 4

    loads = []
    for n, (src, dst) in enumerate(
        ((vel_in, vel.at[pl.ds(0, 96)]), (theta_in, theta), (fz_in, fz), (sz_in, sz), (fy_in, fy), (sy_in, sy))
    ):
        load = pltpu.make_async_copy(src, dst, in_sem.at[n])
        load.start()
        loads.append(load)

    partner = {"blk": 2 * chip + (1 - core)}
    up_blk, down_blk = {"blk": (blk + 1) % 16}, {"blk": (blk + 15) % 16}
    up_row, down_row = {"row": (row + 1) % rows}, {"row": (row + rows - 1) % rows}
    up_col, down_col = {"col": (col + 1) % cols}, {"col": (col + cols - 1) % cols}
    chips, senders = [], []
    for far, dy in ((1, 0), (1, 1), (1, 2), (1, 3), (0, 1), (0, 2), (0, 3)):
        chips.append(((zhi + far) % 2) * 4 + (ypos + dy) % 4)
        senders.append(((zhi + far) % 2) * 4 + (ypos + 4 - dy) % 4)

    barrier = pltpu.get_barrier_semaphore()
    outer = {"blk": (blk + 2 * core + 15) % 16}
    peers = [{"blk": 2 * q + core} for q in chips] + [partner, outer, up_col, down_col]
    peers += [up_row, down_row, {**up_row, **partner}, {**down_row, **partner}]
    for peer in peers:
        pl.semaphore_signal(barrier, inc=1, device_id=peer, device_id_type=pl.DeviceIdType.MESH)
    near_row = jnp.where(zhi == 0, up_row["row"], down_row["row"])
    edge_row = jnp.where(zhi == 0, down_row["row"], up_row["row"])
    at_edge = row == jnp.where(zhi == 0, 0, rows - 1)
    for n in (0, 1):
        owner = {"row": near_row, "blk": 14 * zhi + n}
        pl.semaphore_signal(barrier, inc=1, device_id=owner, device_id_type=pl.DeviceIdType.MESH)

    @pl.when(at_edge)
    def _():
        for n in (0, 1):
            owner = {"row": edge_row, "blk": 14 * (1 - zhi) + n}
            pl.semaphore_signal(barrier, inc=1, device_id=owner, device_id_type=pl.DeviceIdType.MESH)

    owns = (blk <= 1) | (blk >= 14)
    to_row = jnp.where(zhi == 0, down_row["row"], up_row["row"])
    owns_all = owns & (row == jnp.where(zhi == 0, 0, rows - 1))
    expected = len(peers) + jnp.where(owns, 8, 0) + jnp.where(owns_all, 8, 0)

    started = []

    def send(src, dst, ssem, rsem, device):
        copy = pltpu.make_async_remote_copy(
            src_ref=src, dst_ref=dst, send_sem=ssem, recv_sem=rsem,
            device_id=device, device_id_type=pl.DeviceIdType.MESH,
        )
        copy.start()
        started.append(copy)

    def arrived(dst, ssem, rsem, device):
        pltpu.make_async_remote_copy(
            src_ref=dst, dst_ref=dst, send_sem=ssem, recv_sem=rsem,
            device_id=device, device_id_type=pl.DeviceIdType.MESH,
        ).wait_recv()

    vel[pl.ds(96, 32), :] = jnp.zeros((32, 128), F32)
    loads[0].wait()
    vel_t = vel[...].T
    p_row, l_col = iota((128, 128), 0), iota((128, 128), 1)
    plane = p_row & 31
    comp = p_row >> 5
    place = jnp.where(comp == 0, plane & 15, jnp.where(comp == 1, 16 + (plane & 7), 24 + (plane & 7)))
    select = jnp.where((place == (l_col & 31)) & (comp < 3), 1.0, 0.0).astype(BF16)
    k_row, p_lane = iota((8, 128), 0), iota((8, 128), 1)
    plane8 = p_lane & 31
    inside0 = ((plane8 - 4 * k_row + 34) & 31) < 9
    inside1 = ((plane8 - 4 * k_row + 33) & 31) < 7
    lead = p_lane < 32
    window = (lead & inside0) | (jnp.logical_not(lead) & inside1)
    edges = jnp.concatenate(
        [jnp.where(window, jnp.broadcast_to(vel_t[e : e + 1], (8, 128)), 0.0) for e in (0, 1, 126, 127)], axis=0
    )
    picked = sum(dot(piece, select) for piece in split3(edges))
    lane8 = iota((8, 128), 1) >> 5
    nothing = jnp.zeros((8, 128), F32)
    vzpack[0] = jnp.where(lane8 == 2, picked[0:8], jnp.where(lane8 == 3, picked[8:16], nothing))
    vzpack[1] = jnp.where(lane8 == 0, picked[16:24], jnp.where(lane8 == 1, picked[24:32], nothing))
    for q in range(8):
        for base, comp, first, count in ((0, 0, 4 * q - 2, 9), (9, 1, 4 * q - 1, 7), (16, 2, 4 * q - 1, 7)):
            at = 0
            while at < count:
                plane = (first + at) % 32
                take = min(count - at, 32 - plane)
                pack[pl.ds(q * SLAB + base + at, take), :] = vel[pl.ds(comp * 32 + plane, take), :]
                at += take
    loads[1].wait()
    for p in range(4):
        ypack[0, pl.ds(2 * p, 2), :] = theta[p, 0:2, :]
        ypack[1, pl.ds(2 * p, 2), :] = theta[p, 30:32, :]

    def slot(b):
        return pl.ds(pl.multiple_of((b + 2) * SLAB, 8), SLAB)

    def part(first, offset, count):
        return pl.ds(pl.multiple_of(first + offset, 8), count)

    pl.semaphore_wait(barrier, expected)

    send(vzpack.at[1], vzrecv.at[0], v_send.at[0], v_recv.at[0], up_col)
    send(vzpack.at[0], vzrecv.at[1], v_send.at[1], v_recv.at[1], down_col)
    send(ypack.at[1], yrecv.at[0], y_send.at[0], y_recv.at[0], up_row)
    send(ypack.at[0], yrecv.at[1], y_send.at[1], y_recv.at[1], down_row)
    send(theta.at[pl.ds(2, 2)], xlo, x_send.at[0], x_recv.at[0], up_blk)
    send(theta.at[pl.ds(0, 2)], xhi, x_send.at[1], x_recv.at[1], down_blk)
    wown[...] = jnp.concatenate(
        [jnp.full((1, 128), weight[p], F32) for p in range(4)] + [jnp.zeros((4, 128), F32)], axis=0
    )
    send(wown, wlo, w_send.at[0], w_recv.at[0], up_blk)
    send(wown, whi, w_send.at[1], w_recv.at[1], down_blk)
    zpack[0] = theta[:, :, 0:128].reshape(128, 128).T[0:8]
    zpack[1] = theta[:, :, 128:256].reshape(128, 128).T[120:128]
    send(zpack.at[1], zrecv.at[pl.ds(0, 8)], z_send.at[0], z_recv.at[0], up_col)
    send(zpack.at[0], zrecv.at[pl.ds(8, 8)], z_send.at[1], z_recv.at[1], down_col)

    arrived(vzrecv.at[0], v_send.at[0], v_recv.at[0], down_col)
    arrived(vzrecv.at[1], v_send.at[1], v_recv.at[1], up_col)
    edge_rows = vzrecv[0] + vzrecv[1]
    for q in range(8):
        pack[pl.ds(q * SLAB + 23, 1), :] = edge_rows[q : q + 1]

    own_slab = pl.ds(pl.multiple_of(chip * SLAB, 8), SLAB)

    def row_copies(src, side):
        device, place, which = ((up_row, core, core), (down_row, core + 18, core + 2))[side]
        return [
            pltpu.make_async_remote_copy(
                src_ref=src, dst_ref=buf.at[part(place * SLAB, 0, SLAB)],
                send_sem=r_send.at[2 * side + n], recv_sem=r_recv.at[which],
                device_id=where, device_id_type=pl.DeviceIdType.MESH,
            )
            for n, where in enumerate((device, {**device, **partner}))
        ]

    forward_up, forward_down = (zhi == 0) & (row < rows - 1), (zhi == 1) & (row > 0)

    def pass_on(src, q):
        @pl.when((q == 7) & forward_up)
        def _():
            for copy in row_copies(src, 0):
                copy.start()

        @pl.when((q == 0) & forward_down)
        def _():
            for copy in row_copies(src, 1):
                copy.start()

    def owner_copies(half):
        place = jnp.where(zhi == 0, 18, 0) + core
        copies = []
        for n in range(8):
            b = 8 * half + n
            copies.append(pltpu.make_async_remote_copy(
                src_ref=pack.at[part((b // 2) * SLAB, 0, SLAB)], dst_ref=buf.at[part(place * SLAB, 0, SLAB)],
                send_sem=h_send.at[b], recv_sem=r_recv.at[jnp.where(zhi == 0, 2, 0) + core],
                device_id={"row": to_row, "blk": b}, device_id_type=pl.DeviceIdType.MESH,
            ))
        return copies

    for n, q in enumerate(chips):
        send(
            pack.at[part(q * SLAB, 0, SLAB)], buf.at[slot(blk)], a_send.at[n], a_recv.at[n], {"blk": 2 * q + core}
        )
    @pl.when(owns)
    def _():
        for copy in owner_copies(zhi):
            copy.start()

    @pl.when(owns_all)
    def _():
        for copy in owner_copies(1 - zhi):
            copy.start()

    pass_on(pack.at[own_slab], chip)
    send(pack.at[own_slab], buf.at[slot(blk)], p_send.at[7], p_recv.at[7], partner)
    buf[slot(blk), :] = pack[own_slab, :]

    for u in (2, 3, 4):
        loads[u].wait()
    loads[5].wait()
    kk, jj = iota((384, 256), 0), iota((384, 256), 1)
    at = jnp.where(kk < 256, kk, jnp.where(kk < 264, kk - 264, jnp.where(kk < 272, kk - 8, 4096)))
    stencil1, stencil2 = first_weights(at - jj), second_weights(at - jj)
    m1 = sum(dot(stencil1, piece, NT) for piece in split3(fz[...])) * (1.0 / 36.0)
    m1h[...], m1l[...] = split2(m1)
    m2 = sum(dot(stencil2, piece, NT) for piece in split3(sz[...])) * (1.0 / 44.0)
    m2h[...], m2l[...] = split2(m2)
    jy, ly = iota((32, 256), 0), iota((32, 256), 1)
    third = jnp.where(ly < 48, ly, jnp.where(ly < 96, ly - 48, jnp.where(ly < 144, ly - 96, 4096)))
    dy_ = third - 8 - jy
    my1 = sum(dot(piece, first_weights(dy_)) for piece in split3(fy[...])) * (1.0 / 36.0)
    my2 = sum(dot(piece, second_weights(dy_)) for piece in split3(sy[...])) * (1.0 / 44.0)
    both = jnp.concatenate([my1, my2], axis=0)
    high = both.astype(BF16).astype(F32)
    my[...] = jnp.where(iota((64, 256), 1) < 96, high, both - high).astype(BF16)
    kr, zr = iota((256, 384), 0), iota((256, 384), 1)
    group = (kr - 128) >> 5
    cell = jnp.where(kr < 128, kr, jnp.where(group < 2, group - 2, group + 126))
    zz = jnp.where(zr < 256, zr, jnp.where(zr < 264, zr - 264, jnp.where(zr < 272, zr - 8, 4096)))
    near = zz >> 1
    other = near + 2 * (zz & 1) - 1
    rz[...] = jnp.where(cell == near, 0.75, jnp.where(cell == other, 0.25, jnp.zeros((256, 384), F32))).astype(BF16)

    for n in (4, 5, 6):
        b = 2 * senders[n] + core
        arrived(buf.at[slot(b)], a_send.at[n], a_recv.at[n], {"blk": b})
        pass_on(buf.at[slot(b)], senders[n])
        send(buf.at[slot(b)], buf.at[slot(b)], p_send.at[n], p_recv.at[n], partner)
    zrecv[pl.ds(16, 112), :] = jnp.zeros((112, 128), F32)
    for p in range(4):
        tpad[p, 0:8, :] = jnp.zeros((8, 256), F32)
        tpad[p, 40:48, :] = jnp.zeros((8, 256), F32)
        tpad[p, 8:40, :] = theta[p]
    arrived(zrecv.at[pl.ds(0, 8)], z_send.at[0], z_recv.at[0], down_col)
    arrived(zrecv.at[pl.ds(8, 8)], z_send.at[1], z_recv.at[1], up_col)
    side = zrecv[...].T
    th, tl = split2(theta[...].reshape(128, 256))
    sh, sl = split2(side)

    def along_z(mh, ml, ah, al, eh, el):
        high = jnp.concatenate([ah, eh], axis=1)
        low = jnp.concatenate([al, el], axis=1)
        twice = dot(jnp.concatenate([high, low], axis=0), mh)
        return twice[0:128] + twice[128:256] + dot(high, ml)

    gz[...] = along_z(m1h[...], m1l[...], th, tl, sh, sl).reshape(4, 32, 256)
    lap[...] = along_z(m2h[...], m2l[...], th, tl, sh, sl).reshape(4, 32, 256)
    arrived(yrecv.at[0], y_send.at[0], y_recv.at[0], down_row)
    arrived(yrecv.at[1], y_send.at[1], y_recv.at[1], up_row)
    for p in range(4):
        tpad[p, 6:8, :] = yrecv[0, pl.ds(2 * p, 2), :]
        tpad[p, 40:42, :] = yrecv[1, pl.ds(2 * p, 2), :]
        ph, plow = split2(tpad[p])
        res = dot(my[:, 0:144], jnp.concatenate([ph, plow, ph], axis=0))
        gy[p] = res[0:32]
        lap[p] += res[32:64]

    for n in (0, 1, 2, 3):
        b = 2 * senders[n] + core
        arrived(buf.at[slot(b)], a_send.at[n], a_recv.at[n], {"blk": b})
        pass_on(buf.at[slot(b)], senders[n])
        send(buf.at[slot(b)], buf.at[slot(b)], p_send.at[n], p_recv.at[n], partner)
    arrived(wlo, w_send.at[0], w_recv.at[0], down_blk)
    arrived(whi, w_send.at[1], w_recv.at[1], up_blk)
    s_row = iota((16, 128), 0)
    l_row = iota((1, 128), 1) & 31
    for t in range(8):
        low = lower[(4 * blk + t + 62) % 64]
        if t < 2:
            w = wlo[t + 2 : t + 3, :]
        elif t < 6:
            w = wown[t - 2 : t - 1, :]
        else:
            w = whi[t - 6 : t - 5, :]
        s0 = (low - 4 * chip + 34) & 31
        coef[t] = jnp.where(s_row == s0, 1.0 - w, jnp.where(s_row == s0 + 1, w, 0.0))
        for c in range(3):
            if c > 0 and not 2 <= t < 6:
                continue
            if c == 0:
                a0, a1 = low & 15, (low + 1) & 15
            else:
                a0, a1 = 8 + 8 * c + (low & 7), 8 + 8 * c + ((low + 1) & 7)
            line = 8 * c + t
            mix[pl.ds(line, 1), :] = jnp.where(l_row == a0, 1.0 - w, jnp.where(l_row == a1, w, 0.0))
    arrived(xlo, x_send.at[0], x_recv.at[0], down_blk)
    arrived(xhi, x_send.at[1], x_recv.at[1], up_blk)

    def tplane(t):
        if t < 2:
            return xlo[t]
        if t < 6:
            return theta[t - 2]
        return xhi[t - 6]

    for j in range(4):
        t = j + 2
        a, b_, c_, d_, m = tplane(t + 1), tplane(t - 1), tplane(t + 2), tplane(t - 2), tplane(t)
        one = 28.0 * (a - b_) + (c_ - d_)
        two = 48.0 * (a + b_) + 3.0 * (c_ + d_) - 102.0 * m
        for i in range(4):
            s1 = metric[i] * (fx[i, j] * (1.0 / 36.0))
            s2 = metric[i] * metric[i] * (sx[i, j] * (1.0 / 44.0))
            if j == 0:
                gx[i] = s1 * one
            else:
                gx[i] += s1 * one
            lap[i] += s2 * two

    buf[pl.ds(20 * SLAB, 4 * SLAB), :] = jnp.zeros((4 * SLAB, 128), F32)
    for p in range(4):
        fine1[p, 0:8, :] = jnp.zeros((8, 128), F32)
        fine1[p, 40:48, :] = jnp.zeros((8, 128), F32)
    efine[0:8, :] = jnp.zeros((8, 128), F32)
    efine[40:48, :] = jnp.zeros((8, 128), F32)
    for n, q in enumerate(senders):
        arrived(buf.at[slot(2 * q + 1 - core)], p_send.at[n], p_recv.at[n], partner)
    arrived(buf.at[slot(2 * chip + 1 - core)], p_send.at[7], p_recv.at[7], partner)
    for n, place in enumerate((0, 1, 18, 19)):
        arrived(buf.at[pl.ds(place * SLAB, SLAB)], r_send.at[n], r_recv.at[n], up_row)

    def plane_of(line):
        return buf[pl.ds(line, 24, stride=SLAB), :]

    def refine_wide(value, target, n):
        vt[n] = value
        target[pl.ds(6, 18, stride=2), :] = 0.75 * vt[n, 1:19, :] + 0.25 * vt[n, 0:18, :]
        target[pl.ds(7, 18, stride=2), :] = 0.75 * vt[n, 1:19, :] + 0.25 * vt[n, 2:20, :]

    def refine_own(value, target, n):
        vt[n] = value
        target[pl.ds(0, 16, stride=2), :] = 0.75 * vt[n, 2:18, :] + 0.25 * vt[n, 1:17, :]
        target[pl.ds(1, 16, stride=2), :] = 0.75 * vt[n, 2:18, :] + 0.25 * vt[n, 3:19, :]

    refine_wide(plane_of(23), efine, 16)
    edge_wide = efine[...]
    edge_own = efine[8:40, :]
    planes0 = [plane_of(s) for s in range(9)]
    for t in range(8):
        value = coef[t, 0:1, :] * planes0[0]
        for s in range(1, 9):
            value += coef[t, s : s + 1, :] * planes0[s]
        refine_own(value, fine0.at[t], t)
    for c, target, refine in ((1, fine1, refine_wide), (2, fine2, refine_own)):
        planes = [plane_of(2 + 7 * c + s) for s in range(7)]
        for p in range(4):
            value = coef[p + 2, 1:2, :] * planes[0]
            for s in range(1, 7):
                value += coef[p + 2, s + 1 : s + 2, :] * planes[s]
            refine(value, target.at[p], 4 + 4 * c + p)

    lines = [(fine2[p], edge_own, 18 + p) for p in range(4)]
    lines += [(fine1[p], edge_wide, 10 + p) for p in range(4)]
    lines += [(fine0[t], edge_own, t) for t in range(8)]
    interior = jnp.concatenate([one for one, _, _ in lines], axis=0)
    sides = jnp.concatenate([edge * mix[pl.ds(line, 1), :] for _, edge, line in lines], axis=0)
    xh, xl = split2(jnp.concatenate([interior, sides], axis=1))
    flow = dot(xh, rz[:, 0:256]) + dot(xl, rz[:, 0:256])
    flow_side = dot(xh[0:128], rz[:, 256:384]) + dot(xl[0:128], rz[:, 256:384])

    fh, fl = split2(flow[0:128] * theta[...].reshape(128, 256))
    eh, el = split2(flow_side * side)
    total = flow[0:128] * gz[...].reshape(128, 256) + along_z(m1h[...], m1l[...], fh, fl, eh, el)
    out_ref[...] = 0.2 * lap[...] - 0.5 * total.reshape(4, 32, 256)
    for p in range(4):
        flow_y = flow[128 + 48 * p : 176 + 48 * p]
        ph, plow = split2(flow_y * tpad[p])
        slope = dot(my[0:32, 0:144], jnp.concatenate([ph, plow, ph], axis=0))
        own = flow_y[8:40]
        out_ref[p] -= 0.5 * (own * gy[p] + slope) + own
    flows = [flow[320 + 32 * t : 352 + 32 * t] for t in range(8)]
    flux = [flows[t] * tplane(t) for t in range(8)]
    for i in range(4):
        out_ref[i] -= 0.5 * (flows[i + 2] * gx[i])
    for j in range(4):
        t = j + 2
        one = 28.0 * (flux[t + 1] - flux[t - 1]) + (flux[t + 2] - flux[t - 2])
        for i in range(4):
            out_ref[i] -= (0.5 * (metric[i] * (fx[i, j] * (1.0 / 36.0)))) * one

    for copy in started:
        copy.wait_send()

    for side, used in ((0, forward_up), (1, forward_down)):
        @pl.when(used)
        def _(side=side):
            for copy in row_copies(buf.at[pl.ds(0, SLAB)], side):
                copy.wait_send()

    @pl.when(owns)
    def _():
        for copy in owner_copies(zhi):
            copy.wait_send()

    @pl.when(owns_all)
    def _():
        for copy in owner_copies(1 - zhi):
            copy.wait_send()


def local(theta, section, velocity, lower_plane, weight_x, metric_x,
          first_x, first_y, first_z, second_x, second_y, second_z):
    smem = pl.BlockSpec(memory_space=pltpu.SMEM)
    anywhere = pl.BlockSpec(memory_space=pltpu.HBM)

    def vm(*shape, kind=F32):
        return pltpu.VMEM(shape, kind)

    def sem(n):
        return pltpu.SemaphoreType.DMA((n,))

    tendency = pl.pallas_call(
        kernel,
        out_shape=pltpu.VMEM((4, 32, 256), F32),
        in_specs=[smem] * 5 + [anywhere] * 6,
        out_specs=pl.BlockSpec(memory_space=pltpu.VMEM),
        scratch_shapes=[
            vm(4, 32, 256), vm(128, 128), vm(32, 32), vm(32, 32), vm(256, 256), vm(256, 256),
            vm(2, 32, 256), vm(2, 32, 256), vm(8, 128), vm(8, 128), vm(8, 128),
            vm(2, 8, 256), vm(2, 8, 256), vm(2, 8, 128), vm(128, 128), vm(2, 8, 128), vm(2, 8, 128),
            vm(8 * SLAB, 128), vm(24 * SLAB, 128), vm(8, 16, 128), vm(24, 128), vm(256, 384, kind=BF16),
            vm(384, 256, kind=BF16), vm(384, 256, kind=BF16), vm(384, 256, kind=BF16), vm(384, 256, kind=BF16),
            vm(64, 256, kind=BF16), vm(4, 48, 256), vm(17, 24, 128),
            vm(8, 32, 128), vm(4, 48, 128), vm(4, 32, 128), vm(48, 128),
            vm(4, 32, 256), vm(4, 32, 256), vm(4, 32, 256), vm(4, 32, 256),
            sem(6), sem(2), sem(2), sem(2), sem(2), sem(2), sem(2), sem(2), sem(2), sem(2), sem(2),
            sem(7), sem(7), sem(8), sem(8), sem(4), sem(4), sem(16),
        ],
        compiler_params=pltpu.CompilerParams(
            collective_id=0, has_side_effects=True, vmem_limit_bytes=60 * 1024 * 1024
        ),
    )(
        lower_plane, weight_x, metric_x, first_x, second_x,
        theta, velocity.reshape(96, 128), first_y, second_y, first_z, second_z,
    )
    section_new = (-5.0 / 9.0) * section + 0.2 * tendency
    theta_new = theta + (15.0 / 16.0) * section_new
    return (theta_new, section_new)


def solution(mesh):
    placed = (
        P("blk", "row", "col"),
        P("blk", "row", "col"),
        P(None, None, ("row", "blk"), "col"),
        P(),
        P("blk"),
        P("blk"),
        P(),
        P(),
        P(),
        P(),
        P(),
        P(),
    )
    return jax.shard_map(
        local,
        mesh=mesh,
        in_specs=placed,
        out_specs=(P("blk", "row", "col"), P("blk", "row", "col")),
        check_vma=False,
    )
```
